256 devices in a mesh: box: 32 (over z, y), leaf: 8 (over x, core).
Axes of the slice: x: 4, y: 4, z: 8, core: 2. Of those that a mesh axis runs over, the one named last changes fastest.
Arguments:
- sources: bfloat16 [8, 216, 64, 4096], P('leaf', None, None, 'box'), may hold values from -6 to 6
- upward_maps: bfloat16 [8, 216, 216], replicated, may hold values from -0.15625 to 0.15625
- downward_maps: bfloat16 [8, 216, 216], replicated, may hold values from -0.3125 to 0.3125
- cross_maps: bfloat16 [16, 216, 216], replicated, may hold values from -0.1875 to 0.1875
- child_octant: int32 [8, 4096], P('leaf', 'box'), may hold values from 0 to 7
- child_parent: int32 [8, 4096], P('leaf', 'box'), may hold values from 0 to 15
- parent_box: int32 [8, 512], P('leaf', 'box'), may hold values from 0 to 127, as said below
- send_index: int32 [8, 32, 32, 4], P('leaf', 'box'), may hold values from 0 to 127
- near_source: int32 [8, 16, 512], P('leaf', None, 'box'), may hold values from 0 to 127
- near_target: int32 [8, 16, 512], P('leaf', None, 'box'), may hold values from 0 to 127
- far_source: int32 [8, 16, 512], P('leaf', None, 'box'), may hold values from 0 to 127
- far_target: int32 [8, 16, 512], P('leaf', None, 'box'), may hold values from 0 to 127
Outputs:
- expansion: bfloat16 [8, 216, 64, 4096], P('leaf', None, None, 'box')
The draws below stay inside these ranges and needn't reach their ends.
Inputs may be any that keep to these rules, and one draw needn't show every extreme that they name: `parent_box`: within one level and one box device the 16 parent slots name distinct boxes.
All inputs are finite; a program needn't handle non-finite values.
Results may differ from the reference program's by a relative error of at most 0.0095.
Values may be sent and summed in bfloat16 or wider, within the bound.
A program may use at most 128 MiB of HBM per device.

```python
import jax
import jax.numpy as jnp
from jax import lax

Q = 216
W = 64
BOX_DEV = 128
K = 16
BL = 16
BR = 16
LEVELS = 8
NB = 4096
PAR = 16
CAP = 4
N_BOX = 32


def draw_parent_box(key, part):
    key = jax.random.fold_in(key, 11)
    device_count = LEVELS * (NB // BOX_DEV)
    keys = jax.random.split(key, device_count)
    chosen = jax.vmap(lambda one_key: jax.random.permutation(one_key, BOX_DEV)[:PAR])(keys)
    return chosen.reshape(LEVELS, -1).astype(jnp.int32)


def set_ends(entries, own_key, smallest, largest):
    spot = [jax.random.randint(jax.random.fold_in(own_key, axis), (), 0, length) for axis, length in enumerate(entries.shape)]
    main_axis = entries.shape.index(max(entries.shape))
    beside = spot[:main_axis] + [(spot[main_axis] + 1) % entries.shape[main_axis]] + spot[main_axis + 1:]
    return entries.at[tuple(spot)].set(smallest).at[tuple(beside)].set(largest)


def steps_of(key, shape, shards, low, high):
    loudness, own = 1.0, jax.random.fold_in(key, 6)
    for position, blocks in shards:
        draws = jnp.exp(jax.random.uniform(jax.random.fold_in(own, position), (blocks,), jnp.float32, low / len(shards), high / len(shards)))
        loudness = loudness * jnp.repeat(draws, shape[position] // blocks).reshape([-1 if axis == position else 1 for axis in range(len(shape))])
    return loudness


def scatter_about(stream_key, dims, width, most, cuts=(), held_as=jnp.bfloat16):
    values = jax.random.normal(stream_key, dims, jnp.float32) * width
    if len(cuts) > 0:
        values = steps_of(stream_key, dims, cuts, -0.22, 0.18) * values
    return jnp.clip(values, min=-most, max=most).astype(held_as)


def setup_inputs(seed: int = 0) -> dict:
    seeds = jax.random.split(jax.random.key(seed), 13)
    return {
        "sources": scatter_about(seeds[0], (LEVELS, Q, W, NB), 1.0, 6.0, ((0, 8), (3, 32))),
        "upward_maps": scatter_about(seeds[1], (8, Q, Q), (8 * Q) ** -0.5, 0.15625),
        "downward_maps": scatter_about(seeds[2], (8, Q, Q), (2 * Q) ** -0.5, 0.3125),
        "cross_maps": scatter_about(seeds[3], (K, Q, Q), (5 * Q) ** -0.5, 0.1875),
        "child_octant": set_ends(jax.random.randint(seeds[4], (LEVELS, NB), 0, 8), jax.random.fold_in(seeds[4], 1), 0, 7).astype(jnp.int32),
        "child_parent": set_ends(jax.random.randint(seeds[5], (LEVELS, NB), 0, PAR), jax.random.fold_in(seeds[5], 1), 0, PAR - 1).astype(jnp.int32),
        "parent_box": draw_parent_box(jax.random.fold_in(seeds[12], 71), 0),
        "send_index": set_ends(jax.random.randint(seeds[7], (LEVELS, N_BOX, N_BOX, CAP), 0, BOX_DEV), jax.random.fold_in(seeds[7], 1), 0, BOX_DEV - 1).astype(jnp.int32),
        "near_source": set_ends(jax.random.randint(seeds[8], (LEVELS, K, N_BOX * BL), 0, BOX_DEV), jax.random.fold_in(seeds[8], 1), 0, BOX_DEV - 1).astype(jnp.int32),
        "near_target": set_ends(jax.random.randint(seeds[9], (LEVELS, K, N_BOX * BL), 0, BOX_DEV), jax.random.fold_in(seeds[9], 1), 0, BOX_DEV - 1).astype(jnp.int32),
        "far_source": set_ends(jax.random.randint(seeds[10], (LEVELS, K, N_BOX * BR), 0, N_BOX * CAP), jax.random.fold_in(seeds[10], 1), 0, (N_BOX * CAP) - 1).astype(jnp.int32),
        "far_target": set_ends(jax.random.randint(seeds[11], (LEVELS, K, N_BOX * BR), 0, BOX_DEV), jax.random.fold_in(seeds[11], 1), 0, BOX_DEV - 1).astype(jnp.int32),
    }


def translate_up(multipole, octant, parent, upward_maps):
    bucket_index = parent * 8 + octant
    buckets = jnp.zeros((Q, W, PAR * 8), jnp.float32).at[:, :, bucket_index].add(multipole.astype(jnp.float32))
    buckets = buckets.astype(jnp.bfloat16).reshape(Q, W, PAR, 8)
    moved = jnp.einsum("opq,qwro->pwr", upward_maps.astype(jnp.float32), buckets.astype(jnp.float32))
    return moved.astype(jnp.bfloat16)


def absorb(own_density, arrived, parent_slots):
    total = own_density.astype(jnp.float32).at[:, :, parent_slots].add(arrived.astype(jnp.float32))
    return total.astype(jnp.bfloat16)


def translate_down(arrived, downward_maps, octant, parent):
    expanded = jnp.einsum("opq,qwr->pwro", downward_maps.astype(jnp.float32), arrived.astype(jnp.float32))
    expanded = expanded.reshape(Q, W, PAR * 8)
    return jnp.take(expanded, parent * 8 + octant, axis=2)


def translate_pairs(source_pool, pair_source, pair_target, cross_maps):
    def step(total, packed):
        one_map, src, dst = packed
        gathered = jnp.take(source_pool, src, axis=2).astype(jnp.float32)
        moved = jnp.einsum("pq,qwb->pwb", one_map.astype(jnp.float32), gathered)
        return total.at[:, :, dst].add(moved), None

    empty = jnp.zeros((Q, W, BOX_DEV), jnp.float32)
    total, unused = lax.scan(step, empty, (cross_maps, pair_source, pair_target))
    return total


def split_boxes(array):
    return array.reshape(Q, W, N_BOX, BOX_DEV)


def reference(sources, upward_maps, downward_maps, cross_maps, child_octant, child_parent, parent_box, send_index, near_source, near_target, far_source, far_target):
    multipoles = [None] * LEVELS
    multipoles[LEVELS - 1] = sources[LEVELS - 1]
    up_all = jax.vmap(translate_up, in_axes=(2, 0, 0, None), out_axes=2)
    absorb_all = jax.vmap(absorb, in_axes=(2, 2, 0), out_axes=2)
    for level_index in range(LEVELS - 2, -1, -1):
        child = split_boxes(multipoles[level_index + 1])
        octant = child_octant[level_index + 1].reshape(N_BOX, BOX_DEV)
        parent = child_parent[level_index + 1].reshape(N_BOX, BOX_DEV)
        contribution = up_all(child, octant, parent, upward_maps)
        slots = parent_box[level_index].reshape(N_BOX, PAR)
        merged = absorb_all(split_boxes(sources[level_index]), contribution, slots)
        multipoles[level_index] = merged.reshape(Q, W, NB)

    far_fields = []
    for level_index in range(LEVELS):
        split_mult = split_boxes(multipoles[level_index])
        sends = send_index[level_index]
        near_src = jnp.transpose(near_source[level_index].reshape(K, N_BOX, BL), (1, 0, 2))
        near_dst = jnp.transpose(near_target[level_index].reshape(K, N_BOX, BL), (1, 0, 2))
        far_src = jnp.transpose(far_source[level_index].reshape(K, N_BOX, BR), (1, 0, 2))
        far_dst = jnp.transpose(far_target[level_index].reshape(K, N_BOX, BR), (1, 0, 2))

        def one_block(packed):
            block, nsrc, ndst, fsrc, fdst = packed
            wanted = jnp.take(sends, block, axis=1)
            device_rows = jnp.arange(N_BOX, dtype=jnp.int32)[:, None]
            received = split_mult[:, :, device_rows, wanted].reshape(Q, W, N_BOX * CAP)
            own_density = jnp.take(split_mult, block, axis=2)
            source_pool = jnp.concatenate([own_density, received], axis=2)
            pair_source = jnp.concatenate([nsrc, fsrc + BOX_DEV], axis=1)
            pair_target = jnp.concatenate([ndst, fdst], axis=1)
            return translate_pairs(source_pool, pair_source, pair_target, cross_maps)

        blocks = jnp.arange(N_BOX, dtype=jnp.int32)
        field_blocks = lax.map(one_block, (blocks, near_src, near_dst, far_src, far_dst))
        far_fields.append(jnp.transpose(field_blocks, (1, 2, 0, 3)).reshape(Q, W, NB))

    down_all = jax.vmap(translate_down, in_axes=(2, None, 0, 0), out_axes=2)
    take_all = jax.vmap(lambda values, slots: jnp.take(values, slots, axis=2), in_axes=(2, 0), out_axes=2)
    expansions = [far_fields[0].astype(jnp.bfloat16)]
    for level_index in range(1, LEVELS):
        slots = parent_box[level_index - 1].reshape(N_BOX, PAR)
        parent_values = take_all(split_boxes(expansions[level_index - 1]), slots)
        octant = child_octant[level_index].reshape(N_BOX, BOX_DEV)
        parent = child_parent[level_index].reshape(N_BOX, BOX_DEV)
        moved = down_all(parent_values, downward_maps, octant, parent).reshape(Q, W, NB)
        expansions.append((far_fields[level_index] + moved).astype(jnp.bfloat16))
    return jnp.stack(expansions)
```

```python
import functools

import jax
import jax.numpy as jnp
from jax import lax
from jax.experimental import pallas as pl
from jax.experimental.pallas import tpu as pltpu
from jax.sharding import PartitionSpec as P

BF = jnp.bfloat16
F32 = jnp.float32
MESH = pl.DeviceIdType.MESH
QP = 256
CAP = 4


def dot_nn(a, b):
    return lax.dot_general(a, b, (((1,), (0,)), ((), ())), preferred_element_type=F32)


def dot_nt(a, b):
    return lax.dot_general(a, b, (((1,), (1,)), ((), ())), preferred_element_type=F32)


def iota(shape, dim):
    return lax.broadcasted_iota(jnp.int32, shape, dim)


def onehot(mask):
    return mask.astype(F32).astype(BF)


def column_of(table, by_column):
    a, b = table.shape
    n = a * b
    row = iota((n, 1), 0)
    of_a, of_b = (row % a, row // a) if by_column else (row // b, row % b)
    picked = dot_nn(onehot(of_a == iota((n, a), 1)), table.astype(F32).astype(BF))
    return jnp.sum(jnp.where(of_b == iota((n, b), 1), picked, 0.0), axis=1, keepdims=True)


def is_at(column, width):
    return onehot(column == iota((column.shape[0], width), 1).astype(F32))


def kernel(
    dims,
    x_ref, up_ref, down_ref, cross_ref, octant_ref, parent_ref, slots_ref,
    send_index_ref, near_src_ref, near_dst_ref, far_src_ref, far_dst_ref,
    out_ref,
    maps, x32, m_buf, bucket, cin, cout, st, send, recv, gath, moved, far, ein, eout, shift, ost,
    sem_cs, sem_cr, sem_es, sem_er, sem_as, sem_ar, sem_own,
):
    nbox, nleaf, q, w_all, boxes, par, wc, rows_k = dims
    chunks = w_all // wc
    me = lax.axis_index("box")
    level = lax.axis_index("leaf")
    last = nleaf - 1

    barrier = pltpu.get_barrier_semaphore()

    def greet(j, carry):
        pl.semaphore_signal(barrier, inc=1, device_id={"box": lax.rem(me + j, nbox)}, device_id_type=MESH)
        return carry

    lax.fori_loop(1, nbox, greet, 0)

    @pl.when(level > 0)
    def _():
        pl.semaphore_signal(barrier, inc=1, device_id={"leaf": level - 1}, device_id_type=MESH)

    @pl.when(level < last)
    def _():
        pl.semaphore_signal(barrier, inc=1, device_id={"leaf": level + 1}, device_id_type=MESH)

    eye = onehot(iota((boxes, boxes), 0) == iota((boxes, boxes), 1))
    bucket_row = octant_ref[...] * par + parent_ref[...]
    oh_bucket = onehot(bucket_row == iota((8 * par, boxes), 0))
    slot_col = column_of(slots_ref[...], False)
    oh_slot = is_at(slot_col, boxes)
    oh_slot_t = onehot(slots_ref[...] == iota((boxes, par), 0))
    bucket_col = column_of(bucket_row, False)
    oh_bucket_t = is_at(bucket_col, 8 * par)
    oh_send = is_at(column_of(send_index_ref[...], True), boxes)
    oh_near_src = is_at(column_of(near_src_ref[...], False), boxes)
    far_src = far_src_ref[...]
    oh_far_src = is_at(column_of((far_src % CAP) * nbox + far_src // CAP, False), CAP * nbox)
    near_dst_col = column_of(near_dst_ref[...], False)
    far_dst_col = column_of(far_dst_ref[...], False)
    oh_near_dst = is_at(near_dst_col, boxes).astype(F32).T.astype(BF)
    oh_far_dst = is_at(far_dst_col, boxes).astype(F32).T.astype(BF)

    n_up, n_down, n_cross = up_ref.shape[0], down_ref.shape[0], cross_ref.shape[0]

    def pad_maps(source, base, count):
        def one(k, carry):
            maps[base + k] = jnp.zeros((QP, QP), BF)
            maps[base + k, 0:q, 0:q] = source[k]
            return carry
        lax.fori_loop(0, count, one, 0)

    pad_maps(up_ref, 0, n_up)
    pad_maps(down_ref, n_up, n_down)
    pad_maps(cross_ref, n_up + n_down, n_cross)

    x32[q * 16 :, :] = jnp.zeros(((QP - q) * 16, boxes), F32)

    def turn(g, carry):
        x32[0 : q * 16, :] = (
            x_ref[:, pl.ds(pl.multiple_of(g * 16, 16), 16), :].astype(F32).reshape(q * 16, boxes)
        )

        def one(w, inner):
            x_w = x32[pl.ds(w, QP, stride=16), :].astype(BF)
            m_buf[g * 16 + w] = dot_nt(eye, x_w).astype(BF)
            return inner

        lax.fori_loop(0, 16, one, 0, unroll=4)
        return carry

    lax.fori_loop(0, w_all // 16, turn, 0)

    @pl.when(level == last)
    def _():
        cin[...] = jnp.zeros_like(cin)

    @pl.when(level == 0)
    def _():
        ein[...] = jnp.zeros_like(ein)

    pl.semaphore_wait(
        barrier, nbox + 1 - (level == 0).astype(jnp.int32) - (level == last).astype(jnp.int32)
    )

    def chain(buf_from, buf_to, c, s_sem, r_sem, target):
        return pltpu.make_async_remote_copy(
            src_ref=buf_from.at[c], dst_ref=buf_to.at[c], send_sem=s_sem.at[c], recv_sem=r_sem.at[c],
            device_id={"leaf": target}, device_id_type=MESH,
        )

    def upward(c):
        return chain(cout, cin, c, sem_cs, sem_cr, jnp.maximum(level - 1, 0))

    def downward(c):
        return chain(eout, ein, c, sem_es, sem_er, jnp.minimum(level + 1, last))

    def exchange(c, j):
        to = lax.rem(me + j, nbox)
        return pltpu.make_async_remote_copy(
            src_ref=send.at[c, to], dst_ref=recv.at[c, me], send_sem=sem_as.at[c, j],
            recv_sem=sem_ar.at[c, j], device_id={"box": to}, device_id_type=MESH,
        )

    def from_peer(c, j):
        peer = lax.rem(me + nbox - j, nbox)
        return pltpu.make_async_remote_copy(
            src_ref=send.at[c, peer], dst_ref=recv.at[c, peer], send_sem=sem_as.at[c, j],
            recv_sem=sem_ar.at[c, j], device_id={"box": peer}, device_id_type=MESH,
        )

    def own_copy(c):
        return pltpu.make_async_copy(send.at[c, me], recv.at[c, me], sem_own.at[c])

    def up_step(c, carry):
        @pl.when(level < last)
        def _():
            upward(c).wait_recv()

        def merge(w, inner):
            at = c * wc + w
            m_w = (m_buf[at].astype(F32) + dot_nn(oh_slot_t, cin[c, w])).astype(BF)
            m_buf[at] = m_w
            bucket[w] = dot_nn(oh_bucket, m_w).astype(BF)
            return inner

        lax.fori_loop(0, wc, merge, 0, unroll=4)
        total = jnp.zeros((wc * par, QP), F32)
        for o in range(8):
            total += dot_nt(bucket[:, o * par : (o + 1) * par, :].reshape(wc * par, QP), maps[o])
        cout[c] = total.astype(BF).reshape(wc, par, QP)

        @pl.when(level > 0)
        def _():
            upward(c).start()

        def listed(w, inner):
            o_w = dot_nn(oh_send, m_buf[c * wc + w])
            for i in range(CAP):
                for h in range(2):
                    st[h, pl.ds(i * wc + w, nbox, stride=CAP * wc), :] = o_w[
                        i * nbox : (i + 1) * nbox, h * 128 : (h + 1) * 128
                    ]
            return inner

        lax.fori_loop(0, wc, listed, 0, unroll=4)
        for h in range(2):
            send[c, :, :, h * 128 : (h + 1) * 128] = st[h].astype(BF).reshape(nbox, CAP * wc, 128)

        def go(j, inner):
            exchange(c, j).start()
            return inner

        lax.fori_loop(1, nbox, go, 0)
        own_copy(c).start()
        return carry

    lax.fori_loop(0, chunks, up_step, 0)

    def apply_cross():
        def one(k, inner):
            at = pl.multiple_of(k * rows_k, 16)
            moved[:, pl.ds(at, rows_k), :] = (
                dot_nt(gath[:, pl.ds(at, rows_k), :].reshape(wc * rows_k, QP), maps[n_up + n_down + k])
                .astype(BF)
                .reshape(wc, rows_k, QP)
            )
            return inner

        lax.fori_loop(0, n_cross, one, 0, unroll=2)

    def down_step(c, carry):
        def near(w, inner):
            gath[w] = dot_nn(oh_near_src, m_buf[c * wc + w]).astype(BF)
            return inner

        lax.fori_loop(0, wc, near, 0, unroll=4)
        apply_cross()

        def near_add(w, inner):
            far[w] = dot_nn(oh_near_dst, moved[w])
            return inner

        lax.fori_loop(0, wc, near_add, 0, unroll=4)

        def arrived(j, inner):
            from_peer(c, j).wait_recv()
            return inner

        lax.fori_loop(1, nbox, arrived, 0)
        own_copy(c).wait()
        for h in range(2):
            st[h] = recv[c, :, :, h * 128 : (h + 1) * 128].astype(F32).reshape(nbox * CAP * wc, 128)

        def remote(w, inner):
            parts = []
            for i in range(CAP):
                parts.append(
                    jnp.concatenate(
                        [st[h, pl.ds(i * wc + w, nbox, stride=CAP * wc), :] for h in range(2)], axis=1
                    )
                )
            gath[w] = dot_nn(oh_far_src, jnp.concatenate(parts, axis=0).astype(BF)).astype(BF)
            return inner

        lax.fori_loop(0, wc, remote, 0, unroll=4)
        apply_cross()

        def far_add(w, inner):
            far[w] += dot_nn(oh_far_dst, moved[w])
            return inner

        lax.fori_loop(0, wc, far_add, 0, unroll=4)

        @pl.when(level > 0)
        def _():
            downward(c).wait_recv()

        for o in range(8):
            shift[:, o * par : (o + 1) * par, :] = (
                dot_nt(ein[c].reshape(wc * par, QP), maps[n_up + o]).astype(BF).reshape(wc, par, QP)
            )

        def expand(w, inner):
            e_w = (far[w] + dot_nn(oh_bucket_t, shift[w])).astype(BF)
            gath[w, 0:boxes, :] = e_w
            eout[c, w] = dot_nn(oh_slot, e_w).astype(BF)
            return inner

        lax.fori_loop(0, wc, expand, 0, unroll=4)

        @pl.when(level < last)
        def _():
            downward(c).start()

        def back(w, inner):
            e_t = gath[w, 0:boxes, :].astype(F32).T
            ost[pl.ds(lax.rem(c * wc, 16) + w, q, stride=16), :] = e_t[0:q, :]
            return inner

        lax.fori_loop(0, wc, back, 0, unroll=2)

        @pl.when(lax.rem((c + 1) * wc, 16) == 0)
        def _():
            out_ref[:, pl.ds(pl.multiple_of((c * wc) // 16 * 16, 16), 16), :] = (
                ost[...].reshape(q, 16, boxes).astype(BF)
            )

        return carry

    lax.fori_loop(0, chunks, down_step, 0)

    def finish(c, carry):
        def sent(j, inner):
            exchange(c, j).wait_send()
            return inner

        lax.fori_loop(1, nbox, sent, 0)

        @pl.when(level > 0)
        def _():
            upward(c).wait_send()

        @pl.when(level < last)
        def _():
            downward(c).wait_send()

        return carry

    lax.fori_loop(0, chunks, finish, 0)


def per_device(
    sources, upward_maps, downward_maps, cross_maps, child_octant, child_parent, parent_box,
    send_index, near_source, near_target, far_source, far_target,
):
    nbox, nleaf = lax.axis_size("box"), lax.axis_size("leaf")
    _, q, w_all, boxes = sources.shape
    par = parent_box.shape[1]
    rows_k = near_source.shape[2]
    pairs = near_source.shape[1] * rows_k
    wc = 16
    chunks = w_all // wc
    dims = (nbox, nleaf, q, w_all, boxes, par, wc, rows_k)
    n_maps = upward_maps.shape[0] + downward_maps.shape[0] + cross_maps.shape[0]
    dma = pltpu.SemaphoreType.DMA
    out = pl.pallas_call(
        functools.partial(kernel, dims),
        out_shape=jax.ShapeDtypeStruct((q, w_all, boxes), BF),
        in_specs=[pl.BlockSpec(memory_space=pltpu.VMEM)] * 12,
        out_specs=pl.BlockSpec(memory_space=pltpu.VMEM),
        scratch_shapes=[
            pltpu.VMEM((n_maps, QP, QP), BF),
            pltpu.VMEM((QP * 16, boxes), F32),
            pltpu.VMEM((w_all, boxes, QP), BF),
            pltpu.VMEM((wc, 8 * par, QP), BF),
            pltpu.VMEM((chunks, wc, par, QP), BF),
            pltpu.VMEM((chunks, wc, par, QP), BF),
            pltpu.VMEM((2, nbox * CAP * wc, 128), F32),
            pltpu.VMEM((chunks, nbox, CAP * wc, QP), BF),
            pltpu.VMEM((chunks, nbox, CAP * wc, QP), BF),
            pltpu.VMEM((wc, pairs, QP), BF),
            pltpu.VMEM((wc, pairs, QP), BF),
            pltpu.VMEM((wc, boxes, QP), F32),
            pltpu.VMEM((chunks, wc, par, QP), BF),
            pltpu.VMEM((chunks, wc, par, QP), BF),
            pltpu.VMEM((wc, 8 * par, QP), BF),
            pltpu.VMEM((q * 16, boxes), F32),
            dma((chunks,)), dma((chunks,)), dma((chunks,)), dma((chunks,)),
            dma((chunks, nbox)), dma((chunks, nbox)), dma((chunks,)),
        ],
        compiler_params=pltpu.CompilerParams(
            collective_id=0, has_side_effects=True, vmem_limit_bytes=60 * 1024 * 1024
        ),
    )(
        sources[0], upward_maps, downward_maps, cross_maps, child_octant, child_parent, parent_box,
        send_index[0, 0], near_source[0], near_target[0], far_source[0], far_target[0],
    )
    return out[None]


def solution(mesh):
    placed = (
        P("leaf", None, None, "box"),
        P(),
        P(),
        P(),
        P("leaf", "box"),
        P("leaf", "box"),
        P("leaf", "box"),
        P("leaf", "box", None, None),
        P("leaf", None, "box"),
        P("leaf", None, "box"),
        P("leaf", None, "box"),
        P("leaf", None, "box"),
    )
    return jax.shard_map(
        per_device,
        mesh=mesh,
        in_specs=placed,
        out_specs=P("leaf", None, None, "box"),
        check_vma=False,
    )
```

```python
import functools

import jax
import jax.numpy as jnp
from jax import lax
from jax.experimental import pallas as pl
from jax.experimental.pallas import tpu as pltpu
from jax.sharding import PartitionSpec as P

BF = jnp.bfloat16
F32 = jnp.float32
MESH = pl.DeviceIdType.MESH
QP = 256
CAP = 4


def dot_nn(a, b):
    return lax.dot_general(a, b, (((1,), (0,)), ((), ())), preferred_element_type=F32)


def dot_nt(a, b):
    return lax.dot_general(a, b, (((1,), (1,)), ((), ())), preferred_element_type=F32)


def iota(shape, dim):
    return lax.broadcasted_iota(jnp.int32, shape, dim)


def onehot(mask):
    return mask.astype(F32).astype(BF)


def column_of(table, by_column):
    a, b = table.shape
    n = a * b
    row = iota((n, 1), 0)
    of_a, of_b = (row % a, row // a) if by_column else (row // b, row % b)
    picked = dot_nn(onehot(of_a == iota((n, a), 1)), table.astype(F32).astype(BF))
    return jnp.sum(jnp.where(of_b == iota((n, b), 1), picked, 0.0), axis=1, keepdims=True)


def is_at(column, width):
    return onehot(column == iota((column.shape[0], width), 1).astype(F32))


def repeat(count, body, unroll=1):
    def step(index, carry):
        body(index)
        return carry

    lax.fori_loop(0, count, step, 0, unroll=unroll)


def kernel(
    dims,
    x_hbm, up_hbm, down_hbm, cross_hbm, octant_ref, parent_ref, slots_ref,
    send_index_ref, near_src_ref, near_dst_ref, far_src_ref, far_dst_ref,
    out_hbm,
    x_in, up_in, down_in, cross_in, up_maps, down_maps, cross_maps,
    x32, m_buf, x_slot, base, bucket, cin, cout, st, send, recv, gath, moved, far, far_slot,
    ein, eout, shift, ost, out_v,
    sem_in, sem_cs, sem_cr, sem_es, sem_er, sem_as, sem_ar, sem_own, sem_out,
):
    nbox, nleaf, q, w_all, boxes, par, wc, ws, rows_k = dims
    chunks, subs = w_all // wc, wc // ws
    rest = q - 128
    me = lax.axis_index("box")
    level = lax.axis_index("leaf")
    last = nleaf - 1

    barrier = pltpu.get_barrier_semaphore()

    @pl.when(level > 0)
    def _():
        pl.semaphore_signal(barrier, inc=1, device_id={"leaf": level - 1}, device_id_type=MESH)

    @pl.when(level < last)
    def _():
        pl.semaphore_signal(barrier, inc=1, device_id={"leaf": level + 1}, device_id_type=MESH)

    @functools.partial(repeat, nbox - 1)
    def _(j):
        pl.semaphore_signal(
            barrier, inc=1, device_id={"box": lax.rem(me + j + 1, nbox)}, device_id_type=MESH
        )

    def x_copy(c):
        return pltpu.make_async_copy(
            x_hbm.at[:, pl.ds(pl.multiple_of(c * wc, 16), wc), :], x_in.at[c], sem_in.at[c]
        )

    def out_copy(c):
        return pltpu.make_async_copy(
            out_v.at[c], out_hbm.at[:, pl.ds(pl.multiple_of(c * wc, 16), wc), :], sem_out.at[c]
        )

    copy_up = pltpu.make_async_copy(up_hbm, up_in, sem_in.at[chunks])
    copy_down = pltpu.make_async_copy(down_hbm, down_in, sem_in.at[chunks + 1])
    copy_cross = pltpu.make_async_copy(cross_hbm, cross_in, sem_in.at[chunks + 2])
    x_copy(0).start()
    copy_up.start()
    for c in range(1, chunks):
        x_copy(c).start()
    copy_down.start()
    copy_cross.start()

    bucket_row = octant_ref[...] * par + parent_ref[...]
    oh_bucket = onehot(bucket_row == iota((8 * par, boxes), 0))
    oh_slot = is_at(column_of(slots_ref[...], False), boxes)
    oh_slot_t = onehot(slots_ref[...] == iota((boxes, par), 0))
    in_slots = jnp.max(oh_slot.astype(F32), axis=0, keepdims=True)
    oh_bucket_base = (oh_bucket.astype(F32) * (1.0 - in_slots)).astype(BF)
    oh_bucket_slot = dot_nn(oh_bucket, oh_slot_t).astype(BF)
    oh_send = is_at(column_of(send_index_ref[...], False), boxes)

    def turn_maps(source, target, count):
        @functools.partial(repeat, count, unroll=2)
        def _(k):
            target[k] = jnp.zeros((QP, QP), BF)
            target[k, 0:q, 0:q] = source[k].astype(F32).T.astype(BF)

    @pl.when(level == last)
    def _():
        cin[...] = jnp.zeros_like(cin)

    @pl.when(level == 0)
    def _():
        ein[...] = jnp.zeros_like(ein)

    def chain(buf_from, buf_to, c, s_sem, r_sem, target):
        return pltpu.make_async_remote_copy(
            src_ref=buf_from.at[c], dst_ref=buf_to.at[c], send_sem=s_sem.at[c], recv_sem=r_sem.at[c],
            device_id={"leaf": target}, device_id_type=MESH,
        )

    def upward(c):
        return chain(cout, cin, c, sem_cs, sem_cr, jnp.maximum(level - 1, 0))

    def downward(c):
        return chain(eout, ein, c, sem_es, sem_er, jnp.minimum(level + 1, last))

    def exchange(c, j):
        to = lax.rem(me + j, nbox)
        return pltpu.make_async_remote_copy(
            src_ref=send.at[c, to], dst_ref=recv.at[c, me], send_sem=sem_as.at[c, j],
            recv_sem=sem_ar.at[c, j], device_id={"box": to}, device_id_type=MESH,
        )

    def from_peer(c, j):
        peer = lax.rem(me + nbox - j, nbox)
        return pltpu.make_async_remote_copy(
            src_ref=send.at[c, peer], dst_ref=recv.at[c, peer], send_sem=sem_as.at[c, j],
            recv_sem=sem_ar.at[c, j], device_id={"box": peer}, device_id_type=MESH,
        )

    def own_copy(c):
        return pltpu.make_async_copy(send.at[c, me], recv.at[c, me], sem_own.at[c])

    x32[q * wc :, :] = jnp.zeros(((QP - q) * wc, boxes), F32)

    def prepare(c):
        x_copy(c).wait()
        x32[0 : q * wc, :] = x_in[c].astype(F32).reshape(q * wc, boxes)

        @functools.partial(repeat, wc, unroll=8)
        def _(w):
            x_w = x32[pl.ds(w, QP, stride=wc), :].T.astype(BF)
            m_buf[c * wc + w] = x_w
            x_slot[w] = dot_nn(oh_slot, x_w)
            base[w] = dot_nn(oh_bucket_base, x_w)

    def climb(c, s):
        @pl.when(level < last)
        def _():
            upward(c * subs + s).wait_recv()

        for w in range(ws):
            at = s * ws + w
            slot_w = (x_slot[at] + cin[c * subs + s, w].astype(F32)).astype(BF)
            bucket[w] = (base[at] + dot_nn(oh_bucket_slot, slot_w)).astype(BF)
        rows = jnp.concatenate(
            [bucket[:, o * par : (o + 1) * par, :].reshape(ws * par, QP) for o in range(8)], axis=1
        )
        total = dot_nn(rows, up_maps[...].reshape(8 * QP, QP))
        cout[c * subs + s] = total.astype(BF).reshape(ws, par, QP)

        @pl.when(level > 0)
        def _():
            upward(c * subs + s).start()

    lane = iota((nbox, 128), 1)

    def hand_out(c):
        @functools.partial(repeat, wc, unroll=8)
        def _(w):
            at = c * wc + w
            c_w = cin[c * subs + w // ws, w % ws]
            m_w = (m_buf[at].astype(F32) + dot_nn(oh_slot_t, c_w)).astype(BF)
            m_buf[at] = m_w
            o_w = dot_nn(oh_send, m_w)
            tails = []
            for i in range(CAP):
                part = o_w[i * nbox : (i + 1) * nbox]
                st[i, pl.ds(w, nbox, stride=wc), :] = part[:, 0:128]
                tail = part[:, 128:QP]
                tails.append(pltpu.roll(tail, (i * rest) % 128, 1) if i else tail)
            for t in range(CAP - 1):
                packed = jnp.where(lane < (t + 1) * rest - t * 128, tails[t], tails[t + 1])
                st[CAP + t, pl.ds(w, nbox, stride=wc), :] = packed

        for t in range(2 * CAP - 1):
            send[c, :, t * wc : (t + 1) * wc, :] = st[t].astype(BF).reshape(nbox, wc, 128)

        @functools.partial(repeat, nbox - 1)
        def _(j):
            exchange(c, j + 1).start()

        own_copy(c).start()

    copy_up.wait()
    turn_maps(up_in, up_maps, 8)
    prepare(0)
    pl.semaphore_wait(
        barrier, nbox + 1 - (level == 0).astype(jnp.int32) - (level == last).astype(jnp.int32)
    )

    @functools.partial(repeat, chunks)
    def _(c):
        @pl.when(c > 0)
        def _():
            prepare(c)

        for s in range(subs):
            climb(c, s)
        hand_out(c)

    oh_near_src = is_at(column_of(near_src_ref[...], False), boxes)
    far_src = far_src_ref[...]
    oh_far_src = is_at(column_of((far_src % CAP) * nbox + far_src // CAP, False), CAP * nbox)
    near_dst = is_at(column_of(near_dst_ref[...], False), boxes).astype(F32)
    far_dst = is_at(column_of(far_dst_ref[...], False), boxes).astype(F32)
    oh_near_dst = near_dst.T.astype(BF)
    oh_far_dst = far_dst.T.astype(BF)
    oh_near_slot = dot_nn(oh_slot, oh_near_dst).astype(BF)
    oh_far_slot = dot_nn(oh_slot, oh_far_dst).astype(BF)
    oh_bucket_t = oh_bucket.astype(F32).T.astype(BF)
    oh_slot_bucket = dot_nn(oh_slot, oh_bucket_t).astype(BF)
    copy_down.wait()
    turn_maps(down_in, down_maps, 8)
    copy_cross.wait()
    turn_maps(cross_in, cross_maps, cross_in.shape[0])

    def apply_cross():
        @functools.partial(repeat, cross_in.shape[0], unroll=4)
        def _(k):
            at = pl.ds(pl.multiple_of(k * rows_k, 16), rows_k)
            moved[:, at, :] = (
                dot_nn(gath[:, at, :].reshape(wc * rows_k, QP), cross_maps[k])
                .astype(BF)
                .reshape(wc, rows_k, QP)
            )

    def near_field(c):
        @functools.partial(repeat, wc, unroll=8)
        def _(w):
            gath[w] = dot_nn(oh_near_src, m_buf[c * wc + w]).astype(BF)

        apply_cross()

        @functools.partial(repeat, wc, unroll=8)
        def _(w):
            far[w] = dot_nn(oh_near_dst, moved[w])
            far_slot[w] = dot_nn(oh_near_slot, moved[w])

    def far_field(c):
        for t in range(2 * CAP - 1):
            st[t] = recv[c, :, t * wc : (t + 1) * wc, :].astype(F32).reshape(nbox * wc, 128)

        @functools.partial(repeat, wc, unroll=4)
        def _(w):
            tiles = [st[t, pl.ds(w, nbox, stride=wc), :] for t in range(2 * CAP - 1)]
            parts = []
            for i in range(CAP):
                if i == 0:
                    tail = tiles[CAP]
                else:
                    tail = tiles[CAP + i - 1]
                    if i < CAP - 1:
                        tail = jnp.where(lane >= i * rest - (i - 1) * 128, tail, tiles[CAP + i])
                    tail = pltpu.roll(tail, (-i * rest) % 128, 1)
                tail = jnp.where(lane < rest, tail, 0.0)
                parts.append(jnp.concatenate([tiles[i], tail], axis=1))
            gath[w] = dot_nn(oh_far_src, jnp.concatenate(parts, axis=0).astype(BF)).astype(BF)

        apply_cross()

        @functools.partial(repeat, wc, unroll=8)
        def _(w):
            far[w] += dot_nn(oh_far_dst, moved[w])
            far_slot[w] += dot_nn(oh_far_slot, moved[w])

    def descend(c, s):
        @pl.when(level > 0)
        def _():
            downward(c * subs + s).wait_recv()

        rows = ein[c * subs + s].reshape(ws * par, QP)
        for o in range(8):
            shift[s * ws : (s + 1) * ws, o * par : (o + 1) * par, :] = (
                dot_nn(rows, down_maps[o]).astype(BF).reshape(ws, par, QP)
            )
        for w in range(ws):
            at = s * ws + w
            eout[c * subs + s, w] = (far_slot[at] + dot_nn(oh_slot_bucket, shift[at])).astype(BF)

        @pl.when(level < last)
        def _():
            downward(c * subs + s).start()

    def deliver(c):
        @functools.partial(repeat, wc, unroll=4)
        def _(w):
            e_w = far[w] + dot_nn(oh_bucket_t, shift[w])
            ost[pl.ds(w, q, stride=wc), :] = e_w.T[0:q, :]

        out_v[c] = ost[...].reshape(q, wc, boxes).astype(BF)
        out_copy(c).start()

    @functools.partial(repeat, chunks)
    def _(c):
        near_field(c)

        @functools.partial(repeat, nbox - 1)
        def _(j):
            from_peer(c, j + 1).wait_recv()

        own_copy(c).wait()
        far_field(c)
        for s in range(subs):
            descend(c, s)
        deliver(c)

    @functools.partial(repeat, chunks)
    def _(c):
        @functools.partial(repeat, nbox - 1)
        def _(j):
            exchange(c, j + 1).wait_send()

        for s in range(subs):
            @pl.when(level > 0)
            def _():
                upward(c * subs + s).wait_send()

            @pl.when(level < last)
            def _():
                downward(c * subs + s).wait_send()

        out_copy(c).wait()


def copy_kernel(a_ref, b_ref):
    b_ref[...] = a_ref[...]


def per_device(
    sources, upward_maps, downward_maps, cross_maps, child_octant, child_parent, parent_box,
    send_index, near_source, near_target, far_source, far_target,
):
    nbox, nleaf = lax.axis_size("box"), lax.axis_size("leaf")
    _, q, w_all, boxes = sources.shape
    par = parent_box.shape[1]
    rows_k = near_source.shape[2]
    pairs = near_source.shape[1] * rows_k
    wc, ws = 16, 8
    chunks, n_sub = w_all // wc, w_all // ws
    dims = (nbox, nleaf, q, w_all, boxes, par, wc, ws, rows_k)
    dma = pltpu.SemaphoreType.DMA
    any_spec = pl.BlockSpec(memory_space=pl.ANY)
    vmem_spec = pl.BlockSpec(memory_space=pltpu.VMEM)
    n_cross = cross_maps.shape[0]
    out = pl.pallas_call(
        functools.partial(kernel, dims),
        out_shape=jax.ShapeDtypeStruct((q, w_all, boxes), BF),
        in_specs=[any_spec] * 4 + [vmem_spec] * 8,
        out_specs=any_spec,
        scratch_shapes=[
            pltpu.VMEM((chunks, q, wc, boxes), BF),
            pltpu.VMEM(upward_maps.shape, BF),
            pltpu.VMEM(downward_maps.shape, BF),
            pltpu.VMEM(cross_maps.shape, BF),
            pltpu.VMEM((8, QP, QP), BF),
            pltpu.VMEM((8, QP, QP), BF),
            pltpu.VMEM((n_cross, QP, QP), BF),
            pltpu.VMEM((QP * wc, boxes), F32),
            pltpu.VMEM((w_all, boxes, QP), BF),
            pltpu.VMEM((wc, par, QP), F32),
            pltpu.VMEM((wc, 8 * par, QP), F32),
            pltpu.VMEM((ws, 8 * par, QP), BF),
            pltpu.VMEM((n_sub, ws, par, QP), BF),
            pltpu.VMEM((n_sub, ws, par, QP), BF),
            pltpu.VMEM((2 * CAP - 1, nbox * wc, 128), F32),
            pltpu.VMEM((chunks, nbox, (2 * CAP - 1) * wc, 128), BF),
            pltpu.VMEM((chunks, nbox, (2 * CAP - 1) * wc, 128), BF),
            pltpu.VMEM((wc, pairs, QP), BF),
            pltpu.VMEM((wc, pairs, QP), BF),
            pltpu.VMEM((wc, boxes, QP), F32),
            pltpu.VMEM((wc, par, QP), F32),
            pltpu.VMEM((n_sub, ws, par, QP), BF),
            pltpu.VMEM((n_sub, ws, par, QP), BF),
            pltpu.VMEM((wc, 8 * par, QP), BF),
            pltpu.VMEM((q * wc, boxes), F32),
            pltpu.VMEM((chunks, q, wc, boxes), BF),
            dma((chunks + 3,)),
            dma((n_sub,)), dma((n_sub,)), dma((n_sub,)), dma((n_sub,)),
            dma((chunks, nbox)), dma((chunks, nbox)), dma((chunks,)), dma((chunks,)),
        ],
        compiler_params=pltpu.CompilerParams(
            collective_id=0, has_side_effects=True, vmem_limit_bytes=60 * 1024 * 1024
        ),
    )(
        sources[0], upward_maps, downward_maps, cross_maps, child_octant, child_parent, parent_box,
        send_index[0, 0].T, near_source[0], near_target[0], far_source[0], far_target[0],
    )
    block = pl.BlockSpec((q // 9, w_all, boxes), lambda i: (i, 0, 0))
    out = pl.pallas_call(
        copy_kernel,
        grid=(9,),
        out_shape=jax.ShapeDtypeStruct((q, w_all, boxes), BF),
        in_specs=[block],
        out_specs=block,
        compiler_params=pltpu.CompilerParams(vmem_limit_bytes=8 * 1024 * 1024),
    )(out)
    return out[None]


def solution(mesh):
    placed = (
        P("leaf", None, None, "box"),
        P(),
        P(),
        P(),
        P("leaf", "box"),
        P("leaf", "box"),
        P("leaf", "box"),
        P("leaf", "box", None, None),
        P("leaf", None, "box"),
        P("leaf", None, "box"),
        P("leaf", None, "box"),
        P("leaf", None, "box"),
    )
    return jax.shard_map(
        per_device,
        mesh=mesh,
        in_specs=placed,
        out_specs=P("leaf", None, None, "box"),
        check_vma=False,
    )
```

```python
import functools

import jax
import jax.numpy as jnp
from jax import lax
from jax.experimental import pallas as pl
from jax.experimental.pallas import tpu as pltpu
from jax.sharding import PartitionSpec as P

BF = jnp.bfloat16
F32 = jnp.float32
MESH = pl.DeviceIdType.MESH
QP = 256
CAP = 4


def dot_nn(a, b):
    return lax.dot_general(a, b, (((1,), (0,)), ((), ())), preferred_element_type=F32)


def dot_nt(a, b):
    return lax.dot_general(a, b, (((1,), (1,)), ((), ())), preferred_element_type=F32)


def iota(shape, dim):
    return lax.broadcasted_iota(jnp.int32, shape, dim)


def onehot(mask):
    return mask.astype(F32).astype(BF)


def column_of(table, by_column):
    a, b = table.shape
    n = a * b
    row = iota((n, 1), 0)
    of_a, of_b = (row % a, row // a) if by_column else (row // b, row % b)
    picked = dot_nn(onehot(of_a == iota((n, a), 1)), table.astype(F32).astype(BF))
    return jnp.sum(jnp.where(of_b == iota((n, b), 1), picked, 0.0), axis=1, keepdims=True)


def is_at(column, width):
    return onehot(column == iota((column.shape[0], width), 1).astype(F32))


def repeat(count, body, unroll=1):
    def step(index, carry):
        body(index)
        return carry

    lax.fori_loop(0, count, step, 0, unroll=unroll)


def kernel(
    dims,
    x_hbm, up_hbm, down_hbm, cross_hbm, octant_hbm, parent_hbm, slots_hbm,
    send_index_hbm, near_src_hbm, near_dst_hbm, far_src_hbm, far_dst_hbm,
    out_hbm,
    octant_ref, parent_ref, slots_ref,
    send_index_ref, near_src_ref, near_dst_ref, far_src_ref, far_dst_ref,
    x_in, up_in, down_in, cross_in, up_maps, down_maps, cross_maps,
    x32, m_buf, x_slot, base, bucket, cin, cout, st, send, recv, gath, moved, far, far_slot,
    ein, eout, shift, ost, out_v,
    sem_int, sem_in, sem_cs, sem_cr, sem_es, sem_er, sem_as, sem_ar, sem_own, sem_out,
):
    nbox, nleaf, q, w_all, boxes, par, wc, ws, rows_k = dims
    chunks, subs = w_all // wc, wc // ws
    rest = q - 128
    me = lax.axis_index("box")
    level = lax.axis_index("leaf")
    last = nleaf - 1

    barrier = pltpu.get_barrier_semaphore()

    def x_copy(c):
        return pltpu.make_async_copy(
            x_hbm.at[:, pl.ds(pl.multiple_of(c * wc, 16), wc), :], x_in.at[c], sem_in.at[c]
        )

    def out_copy(c):
        return pltpu.make_async_copy(
            out_v.at[c], out_hbm.at[:, pl.ds(pl.multiple_of(c * wc, 16), wc), :], sem_out.at[c]
        )

    copy_up = pltpu.make_async_copy(up_hbm, up_in, sem_in.at[chunks])
    copy_down = pltpu.make_async_copy(down_hbm, down_in, sem_in.at[chunks + 1])
    copy_cross = pltpu.make_async_copy(cross_hbm, cross_in, sem_in.at[chunks + 2])
    int_copies = [
        pltpu.make_async_copy(source, target, sem_int.at[i])
        for i, (source, target) in enumerate(
            (
                (octant_hbm, octant_ref), (parent_hbm, parent_ref), (slots_hbm, slots_ref),
                (send_index_hbm, send_index_ref), (near_src_hbm, near_src_ref),
                (near_dst_hbm, near_dst_ref), (far_src_hbm, far_src_ref), (far_dst_hbm, far_dst_ref),
            )
        )
    ]
    for one in int_copies:
        one.start()
    x_copy(0).start()
    copy_up.start()

    @pl.when(level > 0)
    def _():
        pl.semaphore_signal(barrier, inc=1, device_id={"leaf": level - 1}, device_id_type=MESH)

    @pl.when(level < last)
    def _():
        pl.semaphore_signal(barrier, inc=1, device_id={"leaf": level + 1}, device_id_type=MESH)

    @functools.partial(repeat, nbox - 1)
    def _(j):
        pl.semaphore_signal(
            barrier, inc=1, device_id={"box": lax.rem(me + j + 1, nbox)}, device_id_type=MESH
        )

    for c in range(1, chunks):
        x_copy(c).start()
    copy_down.start()
    copy_cross.start()
    for one in int_copies:
        one.wait()

    bucket_row = octant_ref[...] * par + parent_ref[...]
    oh_bucket = onehot(bucket_row == iota((8 * par, boxes), 0))
    oh_slot = is_at(column_of(slots_ref[...], False), boxes)
    oh_slot_t = onehot(slots_ref[...] == iota((boxes, par), 0))
    in_slots = jnp.max(oh_slot.astype(F32), axis=0, keepdims=True)
    oh_bucket_base = (oh_bucket.astype(F32) * (1.0 - in_slots)).astype(BF)
    oh_bucket_slot = dot_nn(oh_bucket, oh_slot_t).astype(BF)
    oh_send = is_at(column_of(send_index_ref[...], False), boxes)

    def turn_maps(source, target, count):
        @functools.partial(repeat, count, unroll=2)
        def _(k):
            target[k] = jnp.zeros((QP, QP), BF)
            target[k, 0:q, 0:q] = source[k].astype(F32).T.astype(BF)

    @pl.when(level == last)
    def _():
        cin[...] = jnp.zeros_like(cin)

    @pl.when(level == 0)
    def _():
        ein[...] = jnp.zeros_like(ein)

    def chain(buf_from, buf_to, c, s_sem, r_sem, target):
        return pltpu.make_async_remote_copy(
            src_ref=buf_from.at[c], dst_ref=buf_to.at[c], send_sem=s_sem.at[c], recv_sem=r_sem.at[c],
            device_id={"leaf": target}, device_id_type=MESH,
        )

    def upward(c):
        return chain(cout, cin, c, sem_cs, sem_cr, jnp.maximum(level - 1, 0))

    def downward(c):
        return chain(eout, ein, c, sem_es, sem_er, jnp.minimum(level + 1, last))

    def exchange(c, j):
        to = lax.rem(me + j, nbox)
        return pltpu.make_async_remote_copy(
            src_ref=send.at[c, to], dst_ref=recv.at[c, me], send_sem=sem_as.at[c, j],
            recv_sem=sem_ar.at[c, j], device_id={"box": to}, device_id_type=MESH,
        )

    def from_peer(c, j):
        peer = lax.rem(me + nbox - j, nbox)
        return pltpu.make_async_remote_copy(
            src_ref=send.at[c, peer], dst_ref=recv.at[c, peer], send_sem=sem_as.at[c, j],
            recv_sem=sem_ar.at[c, j], device_id={"box": peer}, device_id_type=MESH,
        )

    def own_copy(c):
        return pltpu.make_async_copy(send.at[c, me], recv.at[c, me], sem_own.at[c])

    x32[q * wc :, :] = jnp.zeros(((QP - q) * wc, boxes), F32)

    def prepare(c):
        x_copy(c).wait()
        x32[0 : q * wc, :] = x_in[c].astype(F32).reshape(q * wc, boxes)

        @functools.partial(repeat, wc, unroll=8)
        def _(w):
            x_w = x32[pl.ds(w, QP, stride=wc), :].T.astype(BF)
            m_buf[c * wc + w] = x_w
            x_slot[w] = dot_nn(oh_slot, x_w)
            base[w] = dot_nn(oh_bucket_base, x_w)

    def climb(c, s):
        @pl.when(level < last)
        def _():
            upward(c * subs + s).wait_recv()

        for w in range(ws):
            at = s * ws + w
            slot_w = (x_slot[at] + cin[c * subs + s, w].astype(F32)).astype(BF)
            bucket[w] = (base[at] + dot_nn(oh_bucket_slot, slot_w)).astype(BF)
        rows = jnp.concatenate(
            [bucket[:, o * par : (o + 1) * par, :].reshape(ws * par, QP) for o in range(8)], axis=1
        )
        total = dot_nn(rows, up_maps[...].reshape(8 * QP, QP))
        cout[c * subs + s] = total.astype(BF).reshape(ws, par, QP)

        @pl.when(level > 0)
        def _():
            upward(c * subs + s).start()

    lane = iota((nbox, 128), 1)

    def hand_out(c):
        @functools.partial(repeat, wc, unroll=8)
        def _(w):
            at = c * wc + w
            c_w = cin[c * subs + w // ws, w % ws]
            m_w = (m_buf[at].astype(F32) + dot_nn(oh_slot_t, c_w)).astype(BF)
            m_buf[at] = m_w
            o_w = dot_nn(oh_send, m_w)
            tails = []
            for i in range(CAP):
                part = o_w[i * nbox : (i + 1) * nbox]
                st[i, pl.ds(w, nbox, stride=wc), :] = part[:, 0:128]
                tail = part[:, 128:QP]
                tails.append(pltpu.roll(tail, (i * rest) % 128, 1) if i else tail)
            for t in range(CAP - 1):
                packed = jnp.where(lane < (t + 1) * rest - t * 128, tails[t], tails[t + 1])
                st[CAP + t, pl.ds(w, nbox, stride=wc), :] = packed

        for t in range(2 * CAP - 1):
            send[c, :, t * wc : (t + 1) * wc, :] = st[t].astype(BF).reshape(nbox, wc, 128)

        @functools.partial(repeat, nbox - 1)
        def _(j):
            exchange(c, j + 1).start()

        own_copy(c).start()

    copy_up.wait()
    turn_maps(up_in, up_maps, 8)
    prepare(0)
    pl.semaphore_wait(
        barrier, nbox + 1 - (level == 0).astype(jnp.int32) - (level == last).astype(jnp.int32)
    )

    @functools.partial(repeat, chunks)
    def _(c):
        @pl.when(c > 0)
        def _():
            prepare(c)

        for s in range(subs):
            climb(c, s)
        hand_out(c)

    oh_near_src = is_at(column_of(near_src_ref[...], False), boxes)
    far_src = far_src_ref[...]
    oh_far_src = is_at(column_of((far_src % CAP) * nbox + far_src // CAP, False), CAP * nbox)
    near_dst = is_at(column_of(near_dst_ref[...], False), boxes).astype(F32)
    far_dst = is_at(column_of(far_dst_ref[...], False), boxes).astype(F32)
    oh_near_dst = near_dst.T.astype(BF)
    oh_far_dst = far_dst.T.astype(BF)
    oh_near_slot = dot_nn(oh_slot, oh_near_dst).astype(BF)
    oh_far_slot = dot_nn(oh_slot, oh_far_dst).astype(BF)
    oh_bucket_t = oh_bucket.astype(F32).T.astype(BF)
    oh_slot_bucket = dot_nn(oh_slot, oh_bucket_t).astype(BF)
    copy_down.wait()
    turn_maps(down_in, down_maps, 8)
    copy_cross.wait()
    turn_maps(cross_in, cross_maps, cross_in.shape[0])

    def apply_cross():
        @functools.partial(repeat, cross_in.shape[0], unroll=4)
        def _(k):
            at = pl.ds(pl.multiple_of(k * rows_k, 16), rows_k)
            moved[:, at, :] = (
                dot_nn(gath[:, at, :].reshape(wc * rows_k, QP), cross_maps[k])
                .astype(BF)
                .reshape(wc, rows_k, QP)
            )

    def near_field(c):
        @functools.partial(repeat, wc, unroll=8)
        def _(w):
            gath[w] = dot_nn(oh_near_src, m_buf[c * wc + w]).astype(BF)

        apply_cross()

        @functools.partial(repeat, wc, unroll=8)
        def _(w):
            far[w] = dot_nn(oh_near_dst, moved[w])
            far_slot[w] = dot_nn(oh_near_slot, moved[w])

    def far_field(c):
        for t in range(2 * CAP - 1):
            st[t] = recv[c, :, t * wc : (t + 1) * wc, :].astype(F32).reshape(nbox * wc, 128)

        @functools.partial(repeat, wc, unroll=8)
        def _(w):
            tiles = [st[t, pl.ds(w, nbox, stride=wc), :] for t in range(2 * CAP - 1)]
            parts = []
            for i in range(CAP):
                if i == 0:
                    tail = tiles[CAP]
                else:
                    tail = tiles[CAP + i - 1]
                    if i < CAP - 1:
                        tail = jnp.where(lane >= i * rest - (i - 1) * 128, tail, tiles[CAP + i])
                    tail = pltpu.roll(tail, (-i * rest) % 128, 1)
                tail = jnp.where(lane < rest, tail, 0.0)
                parts.append(jnp.concatenate([tiles[i], tail], axis=1))
            gath[w] = dot_nn(oh_far_src, jnp.concatenate(parts, axis=0).astype(BF)).astype(BF)

        apply_cross()

        @functools.partial(repeat, wc, unroll=8)
        def _(w):
            far[w] += dot_nn(oh_far_dst, moved[w])
            far_slot[w] += dot_nn(oh_far_slot, moved[w])

    def descend(c, s):
        @pl.when(level > 0)
        def _():
            downward(c * subs + s).wait_recv()

        rows = ein[c * subs + s].reshape(ws * par, QP)
        for o in range(8):
            shift[s * ws : (s + 1) * ws, o * par : (o + 1) * par, :] = (
                dot_nn(rows, down_maps[o]).astype(BF).reshape(ws, par, QP)
            )
        for w in range(ws):
            at = s * ws + w
            eout[c * subs + s, w] = (far_slot[at] + dot_nn(oh_slot_bucket, shift[at])).astype(BF)

        @pl.when(level < last)
        def _():
            downward(c * subs + s).start()

    def deliver(c):
        @functools.partial(repeat, wc, unroll=8)
        def _(w):
            e_w = far[w] + dot_nn(oh_bucket_t, shift[w])
            ost[pl.ds(w, q, stride=wc), :] = e_w.T[0:q, :]

        out_v[c] = ost[...].reshape(q, wc, boxes).astype(BF)
        out_copy(c).start()

    @functools.partial(repeat, chunks)
    def _(c):
        near_field(c)

        @functools.partial(repeat, nbox - 1)
        def _(j):
            from_peer(c, j + 1).wait_recv()

        own_copy(c).wait()
        far_field(c)
        for s in range(subs):
            descend(c, s)
        deliver(c)

    @functools.partial(repeat, chunks)
    def _(c):
        @functools.partial(repeat, nbox - 1)
        def _(j):
            exchange(c, j + 1).wait_send()

        for s in range(subs):
            @pl.when(level > 0)
            def _():
                upward(c * subs + s).wait_send()

            @pl.when(level < last)
            def _():
                downward(c * subs + s).wait_send()

        out_copy(c).wait()


def copy_kernel(parts, a_ref, b_ref, held, sems):
    size = a_ref.shape[0] // parts
    at = [pl.ds(i * size, size) for i in range(parts)]
    inward = [pltpu.make_async_copy(a_ref.at[at[i]], held.at[at[i]], sems.at[0, i]) for i in range(parts)]
    outward = [pltpu.make_async_copy(held.at[at[i]], b_ref.at[at[i]], sems.at[1, i]) for i in range(parts)]
    for one in inward:
        one.start()
    for i in range(parts):
        inward[i].wait()
        outward[i].start()
    for one in outward:
        one.wait()


def per_device(
    sources, upward_maps, downward_maps, cross_maps, child_octant, child_parent, parent_box,
    send_index, near_source, near_target, far_source, far_target,
):
    nbox, nleaf = lax.axis_size("box"), lax.axis_size("leaf")
    _, q, w_all, boxes = sources.shape
    par = parent_box.shape[1]
    rows_k = near_source.shape[2]
    pairs = near_source.shape[1] * rows_k
    wc, ws = 16, 4
    chunks, n_sub = w_all // wc, w_all // ws
    dims = (nbox, nleaf, q, w_all, boxes, par, wc, ws, rows_k)
    integers = (
        child_octant, child_parent, parent_box, send_index[0, 0].T,
        near_source[0], near_target[0], far_source[0], far_target[0],
    )
    dma = pltpu.SemaphoreType.DMA
    any_spec = pl.BlockSpec(memory_space=pl.ANY)
    n_cross = cross_maps.shape[0]
    out = pl.pallas_call(
        functools.partial(kernel, dims),
        out_shape=jax.ShapeDtypeStruct((q, w_all, boxes), BF),
        in_specs=[any_spec] * 12,
        out_specs=any_spec,
        scratch_shapes=[pltpu.VMEM(one.shape, jnp.int32) for one in integers]
        + [
            pltpu.VMEM((chunks, q, wc, boxes), BF),
            pltpu.VMEM(upward_maps.shape, BF),
            pltpu.VMEM(downward_maps.shape, BF),
            pltpu.VMEM(cross_maps.shape, BF),
            pltpu.VMEM((8, QP, QP), BF),
            pltpu.VMEM((8, QP, QP), BF),
            pltpu.VMEM((n_cross, QP, QP), BF),
            pltpu.VMEM((QP * wc, boxes), F32),
            pltpu.VMEM((w_all, boxes, QP), BF),
            pltpu.VMEM((wc, par, QP), F32),
            pltpu.VMEM((wc, 8 * par, QP), F32),
            pltpu.VMEM((ws, 8 * par, QP), BF),
            pltpu.VMEM((n_sub, ws, par, QP), BF),
            pltpu.VMEM((n_sub, ws, par, QP), BF),
            pltpu.VMEM((2 * CAP - 1, nbox * wc, 128), F32),
            pltpu.VMEM((chunks, nbox, (2 * CAP - 1) * wc, 128), BF),
            pltpu.VMEM((chunks, nbox, (2 * CAP - 1) * wc, 128), BF),
            pltpu.VMEM((wc, pairs, QP), BF),
            pltpu.VMEM((wc, pairs, QP), BF),
            pltpu.VMEM((wc, boxes, QP), F32),
            pltpu.VMEM((wc, par, QP), F32),
            pltpu.VMEM((n_sub, ws, par, QP), BF),
            pltpu.VMEM((n_sub, ws, par, QP), BF),
            pltpu.VMEM((wc, 8 * par, QP), BF),
            pltpu.VMEM((q * wc, boxes), F32),
            pltpu.VMEM((chunks, q, wc, boxes), BF),
            dma((len(integers),)), dma((chunks + 3,)),
            dma((n_sub,)), dma((n_sub,)), dma((n_sub,)), dma((n_sub,)),
            dma((chunks, nbox)), dma((chunks, nbox)), dma((chunks,)), dma((chunks,)),
        ],
        compiler_params=pltpu.CompilerParams(
            collective_id=0, has_side_effects=True, vmem_limit_bytes=60 * 1024 * 1024
        ),
    )(
        sources[0], upward_maps, downward_maps, cross_maps, *integers
    )
    parts = 8
    out = pl.pallas_call(
        functools.partial(copy_kernel, parts),
        out_shape=jax.ShapeDtypeStruct((q, w_all, boxes), BF),
        in_specs=[any_spec],
        out_specs=any_spec,
        scratch_shapes=[pltpu.VMEM((q, w_all, boxes), BF), dma((2, parts))],
        compiler_params=pltpu.CompilerParams(vmem_limit_bytes=60 * 1024 * 1024),
    )(out)
    return out[None]


def solution(mesh):
    placed = (
        P("leaf", None, None, "box"),
        P(),
        P(),
        P(),
        P("leaf", "box"),
        P("leaf", "box"),
        P("leaf", "box"),
        P("leaf", "box", None, None),
        P("leaf", None, "box"),
        P("leaf", None, "box"),
        P("leaf", None, "box"),
        P("leaf", None, "box"),
    )
    return jax.shard_map(
        per_device,
        mesh=mesh,
        in_specs=placed,
        out_specs=P("leaf", None, None, "box"),
        check_vma=False,
    )
```

```python
import functools

import jax
import jax.numpy as jnp
from jax import lax
from jax.experimental import pallas as pl
from jax.experimental.pallas import tpu as pltpu
from jax.sharding import PartitionSpec as P

BF = jnp.bfloat16
F32 = jnp.float32
MESH = pl.DeviceIdType.MESH
QP = 256
CAP = 4
RELAYS = (2, 0)


def dot_nn(a, b):
    return lax.dot_general(a, b, (((1,), (0,)), ((), ())), preferred_element_type=F32)


def dot_nt(a, b):
    return lax.dot_general(a, b, (((1,), (1,)), ((), ())), preferred_element_type=F32)


def iota(shape, dim):
    return lax.broadcasted_iota(jnp.int32, shape, dim)


def onehot(mask):
    return mask.astype(F32).astype(BF)


def column_of(table, by_column):
    a, b = table.shape
    n = a * b
    row = iota((n, 1), 0)
    of_a, of_b = (row % a, row // a) if by_column else (row // b, row % b)
    picked = dot_nn(onehot(of_a == iota((n, a), 1)), table.astype(F32).astype(BF))
    return jnp.sum(jnp.where(of_b == iota((n, b), 1), picked, 0.0), axis=1, keepdims=True)


def is_at(column, width):
    return onehot(column == iota((column.shape[0], width), 1).astype(F32))


def repeat(count, body, unroll=1):
    def step(index, carry):
        body(index)
        return carry

    lax.fori_loop(0, count, step, 0, unroll=unroll)


def kernel(
    dims,
    x_hbm, up_hbm, down_hbm, cross_hbm, octant_hbm, parent_hbm, slots_hbm,
    send_index_hbm, near_src_hbm, near_dst_hbm, far_src_hbm, far_dst_hbm,
    out_hbm,
    octant_ref, parent_ref, slots_ref,
    send_index_ref, near_src_ref, near_dst_ref, far_src_ref, far_dst_ref,
    x_in, up_in, down_in, cross_in, up_maps, down_maps, cross_maps,
    x32, m_buf, x_slot, base, bucket, cin, cout, st, send, recv, gath, moved, far, far_slot,
    ein, eout, shift, ost, out_v, relay,
    sem_int, sem_in, sem_cs, sem_cr, sem_es, sem_er, sem_as, sem_ar, sem_own, sem_out, sem_rs, sem_rr,
):
    nbox, nleaf, q, w_all, boxes, par, wc, ws, rows_k = dims
    chunks, subs = w_all // wc, wc // ws
    rest = q - 128
    me = lax.axis_index("box")
    level = lax.axis_index("leaf")
    last = nleaf - 1
    mirror = nleaf - 2 - level // 2 * 2 + level % 2
    relayed = [nbox // 2, nbox // 2 + 1, nbox // 2 - 1][: RELAYS[0]]
    hands_over = [level < 2 * sum(n > r for n in RELAYS) for r in range(len(relayed))]
    carries = [level >= nleaf - 2 * sum(n > r for n in RELAYS) for r in range(len(relayed))]

    barrier = pltpu.get_barrier_semaphore()

    def greet_mirror(offset):
        pl.semaphore_signal(
            barrier, inc=1, device_id={"box": lax.rem(me + nbox + offset, nbox), "leaf": mirror},
            device_id_type=MESH,
        )

    def x_copy(c):
        return pltpu.make_async_copy(
            x_hbm.at[:, pl.ds(pl.multiple_of(c * wc, 16), wc), :], x_in.at[c], sem_in.at[c]
        )

    def out_copy(c):
        return pltpu.make_async_copy(
            out_v.at[c], out_hbm.at[:, pl.ds(pl.multiple_of(c * wc, 16), wc), :], sem_out.at[c]
        )

    copy_up = pltpu.make_async_copy(up_hbm, up_in, sem_in.at[chunks])
    copy_down = pltpu.make_async_copy(down_hbm, down_in, sem_in.at[chunks + 1])
    copy_cross = pltpu.make_async_copy(cross_hbm, cross_in, sem_in.at[chunks + 2])
    int_copies = [
        pltpu.make_async_copy(source, target, sem_int.at[i])
        for i, (source, target) in enumerate(
            (
                (octant_hbm, octant_ref), (parent_hbm, parent_ref), (slots_hbm, slots_ref),
                (send_index_hbm, send_index_ref), (near_src_hbm, near_src_ref),
                (near_dst_hbm, near_dst_ref), (far_src_hbm, far_src_ref), (far_dst_hbm, far_dst_ref),
            )
        )
    ]
    for one in int_copies:
        one.start()
    x_copy(0).start()
    copy_up.start()

    @pl.when(level > 0)
    def _():
        pl.semaphore_signal(barrier, inc=1, device_id={"leaf": level - 1}, device_id_type=MESH)

    @pl.when(level < last)
    def _():
        pl.semaphore_signal(barrier, inc=1, device_id={"leaf": level + 1}, device_id_type=MESH)

    @functools.partial(repeat, nbox - 1)
    def _(j):
        pl.semaphore_signal(
            barrier, inc=1, device_id={"box": lax.rem(me + j + 1, nbox)}, device_id_type=MESH
        )

    expected = nbox + 1 - (level == 0).astype(jnp.int32) - (level == last).astype(jnp.int32)
    for r, offset in enumerate(relayed):
        expected += (hands_over[r] | carries[r]).astype(jnp.int32) * (2 if r == 0 else 1)

        @pl.when(hands_over[r])
        def _():
            greet_mirror(-offset)
            if r == 0:
                greet_mirror(0)

        @pl.when(carries[r])
        def _():
            greet_mirror(offset)
            if r == 0:
                greet_mirror(0)

    for c in range(1, chunks):
        x_copy(c).start()
    copy_down.start()
    copy_cross.start()
    for one in int_copies:
        one.wait()

    bucket_row = octant_ref[...] * par + parent_ref[...]
    oh_bucket = onehot(bucket_row == iota((8 * par, boxes), 0))
    oh_slot = is_at(column_of(slots_ref[...], False), boxes)
    oh_slot_t = onehot(slots_ref[...] == iota((boxes, par), 0))
    in_slots = jnp.max(oh_slot.astype(F32), axis=0, keepdims=True)
    oh_bucket_base = (oh_bucket.astype(F32) * (1.0 - in_slots)).astype(BF)
    oh_bucket_slot = dot_nn(oh_bucket, oh_slot_t).astype(BF)
    oh_send = is_at(column_of(send_index_ref[...], False), boxes)

    def turn_maps(source, target, count):
        @functools.partial(repeat, count, unroll=2)
        def _(k):
            target[k] = jnp.zeros((QP, QP), BF)
            target[k, 0:q, 0:q] = source[k].astype(F32).T.astype(BF)

    @pl.when(level == last)
    def _():
        cin[...] = jnp.zeros_like(cin)

    @pl.when(level == 0)
    def _():
        ein[...] = jnp.zeros_like(ein)

    def chain(buf_from, buf_to, c, s_sem, r_sem, target):
        return pltpu.make_async_remote_copy(
            src_ref=buf_from.at[c], dst_ref=buf_to.at[c], send_sem=s_sem.at[c], recv_sem=r_sem.at[c],
            device_id={"leaf": target}, device_id_type=MESH,
        )

    def upward(c):
        return chain(cout, cin, c, sem_cs, sem_cr, jnp.maximum(level - 1, 0))

    def downward(c):
        return chain(eout, ein, c, sem_es, sem_er, jnp.minimum(level + 1, last))

    def exchange(c, j):
        to = lax.rem(me + j, nbox)
        return pltpu.make_async_remote_copy(
            src_ref=send.at[c, to], dst_ref=recv.at[c, me], send_sem=sem_as.at[c, j],
            recv_sem=sem_ar.at[c, j], device_id={"box": to}, device_id_type=MESH,
        )

    def from_peer(c, j):
        peer = lax.rem(me + nbox - j, nbox)
        return pltpu.make_async_remote_copy(
            src_ref=send.at[c, peer], dst_ref=recv.at[c, peer], send_sem=sem_as.at[c, j],
            recv_sem=sem_ar.at[c, j], device_id={"box": peer}, device_id_type=MESH,
        )

    def hand_over(c, r):
        to = lax.rem(me + relayed[r], nbox)
        return pltpu.make_async_remote_copy(
            src_ref=send.at[c, to], dst_ref=relay.at[c, r], send_sem=sem_as.at[c, relayed[r]],
            recv_sem=sem_rr.at[c, r], device_id={"leaf": mirror}, device_id_type=MESH,
        )

    def carry_on(c, r):
        to = lax.rem(me + relayed[r], nbox)
        return pltpu.make_async_remote_copy(
            src_ref=relay.at[c, r], dst_ref=recv.at[c, me], send_sem=sem_rs.at[c, r],
            recv_sem=sem_ar.at[c, relayed[r]], device_id={"box": to, "leaf": mirror}, device_id_type=MESH,
        )

    def forward(c):
        for r in range(len(relayed)):
            @pl.when(carries[r])
            def _():
                hand_over(c, r).wait_recv()
                carry_on(c, r).start()

    def own_copy(c):
        return pltpu.make_async_copy(send.at[c, me], recv.at[c, me], sem_own.at[c])

    x32[q * wc :, :] = jnp.zeros(((QP - q) * wc, boxes), F32)

    def prepare(c):
        x_copy(c).wait()
        x32[0 : q * wc, :] = x_in[c].astype(F32).reshape(q * wc, boxes)

        @functools.partial(repeat, wc, unroll=8)
        def _(w):
            x_w = x32[pl.ds(w, QP, stride=wc), :].T.astype(BF)
            m_buf[c * wc + w] = x_w
            x_slot[w] = dot_nn(oh_slot, x_w)
            base[w] = dot_nn(oh_bucket_base, x_w)

    def climb(c, s):
        @pl.when(level < last)
        def _():
            upward(c * subs + s).wait_recv()

        for w in range(ws):
            at = s * ws + w
            slot_w = (x_slot[at] + cin[c * subs + s, w].astype(F32)).astype(BF)
            bucket[w] = (base[at] + dot_nn(oh_bucket_slot, slot_w)).astype(BF)
        rows = jnp.concatenate(
            [bucket[:, o * par : (o + 1) * par, :].reshape(ws * par, QP) for o in range(8)], axis=1
        )
        total = dot_nn(rows, up_maps[...].reshape(8 * QP, QP))
        cout[c * subs + s] = total.astype(BF).reshape(ws, par, QP)

        @pl.when(level > 0)
        def _():
            upward(c * subs + s).start()

    lane = iota((nbox, 128), 1)

    def send_direct(c):
        @functools.partial(repeat, nbox - 1)
        def _(j):
            direct = j >= 0
            for r, offset in enumerate(relayed):
                direct &= jnp.logical_not(hands_over[r] & (j + 1 == offset))

            @pl.when(direct)
            def _():
                exchange(c, j + 1).start()

    def hand_out(c):
        @functools.partial(repeat, wc, unroll=8)
        def _(w):
            at = c * wc + w
            c_w = cin[c * subs + w // ws, w % ws]
            m_w = (m_buf[at].astype(F32) + dot_nn(oh_slot_t, c_w)).astype(BF)
            m_buf[at] = m_w
            o_w = dot_nn(oh_send, m_w)
            tails = []
            for i in range(CAP):
                part = o_w[i * nbox : (i + 1) * nbox]
                st[i, pl.ds(w, nbox, stride=wc), :] = part[:, 0:128]
                tail = part[:, 128:QP]
                tails.append(pltpu.roll(tail, (i * rest) % 128, 1) if i else tail)
            for t in range(CAP - 1):
                packed = jnp.where(lane < (t + 1) * rest - t * 128, tails[t], tails[t + 1])
                st[CAP + t, pl.ds(w, nbox, stride=wc), :] = packed

        for t in range(2 * CAP - 1):
            send[c, :, t * wc : (t + 1) * wc, :] = st[t].astype(BF).reshape(nbox, wc, 128)

        for r in range(len(relayed)):
            @pl.when(hands_over[r])
            def _():
                hand_over(c, r).start()

        @pl.when(jnp.logical_not(carries[0]) | (c == 0))
        def _():
            send_direct(c)

        own_copy(c).start()

    copy_up.wait()
    turn_maps(up_in, up_maps, 8)
    prepare(0)
    pl.semaphore_wait(barrier, expected)

    @functools.partial(repeat, chunks)
    def _(c):
        @pl.when(c > 0)
        def _():
            prepare(c)

        for s in range(subs):
            climb(c, s)
        hand_out(c)

    oh_near_src = is_at(column_of(near_src_ref[...], False), boxes)
    far_src = far_src_ref[...]
    oh_far_src = is_at(column_of((far_src % CAP) * nbox + far_src // CAP, False), CAP * nbox)
    near_dst = is_at(column_of(near_dst_ref[...], False), boxes).astype(F32)
    far_dst = is_at(column_of(far_dst_ref[...], False), boxes).astype(F32)
    oh_near_dst = near_dst.T.astype(BF)
    oh_far_dst = far_dst.T.astype(BF)
    oh_near_slot = dot_nn(oh_slot, oh_near_dst).astype(BF)
    oh_far_slot = dot_nn(oh_slot, oh_far_dst).astype(BF)
    oh_bucket_t = oh_bucket.astype(F32).T.astype(BF)
    oh_slot_bucket = dot_nn(oh_slot, oh_bucket_t).astype(BF)
    copy_down.wait()
    turn_maps(down_in, down_maps, 8)
    copy_cross.wait()
    turn_maps(cross_in, cross_maps, cross_in.shape[0])

    def apply_cross():
        @functools.partial(repeat, cross_in.shape[0], unroll=4)
        def _(k):
            at = pl.ds(pl.multiple_of(k * rows_k, 16), rows_k)
            moved[:, at, :] = (
                dot_nn(gath[:, at, :].reshape(wc * rows_k, QP), cross_maps[k])
                .astype(BF)
                .reshape(wc, rows_k, QP)
            )

    def near_field(c):
        @functools.partial(repeat, wc, unroll=8)
        def _(w):
            gath[w] = dot_nn(oh_near_src, m_buf[c * wc + w]).astype(BF)

        apply_cross()

        @functools.partial(repeat, wc, unroll=8)
        def _(w):
            far[w] = dot_nn(oh_near_dst, moved[w])
            far_slot[w] = dot_nn(oh_near_slot, moved[w])

    def far_field(c):
        for t in range(2 * CAP - 1):
            st[t] = recv[c, :, t * wc : (t + 1) * wc, :].astype(F32).reshape(nbox * wc, 128)

        @functools.partial(repeat, wc, unroll=8)
        def _(w):
            tiles = [st[t, pl.ds(w, nbox, stride=wc), :] for t in range(2 * CAP - 1)]
            parts = []
            for i in range(CAP):
                if i == 0:
                    tail = tiles[CAP]
                else:
                    tail = tiles[CAP + i - 1]
                    if i < CAP - 1:
                        tail = jnp.where(lane >= i * rest - (i - 1) * 128, tail, tiles[CAP + i])
                    tail = pltpu.roll(tail, (-i * rest) % 128, 1)
                tail = jnp.where(lane < rest, tail, 0.0)
                parts.append(jnp.concatenate([tiles[i], tail], axis=1))
            gath[w] = dot_nn(oh_far_src, jnp.concatenate(parts, axis=0).astype(BF)).astype(BF)

        apply_cross()

        @functools.partial(repeat, wc, unroll=8)
        def _(w):
            far[w] += dot_nn(oh_far_dst, moved[w])
            far_slot[w] += dot_nn(oh_far_slot, moved[w])

    def descend(c, s):
        @pl.when(level > 0)
        def _():
            downward(c * subs + s).wait_recv()

        rows = ein[c * subs + s].reshape(ws * par, QP)
        for o in range(8):
            shift[s * ws : (s + 1) * ws, o * par : (o + 1) * par, :] = (
                dot_nn(rows, down_maps[o]).astype(BF).reshape(ws, par, QP)
            )
        for w in range(ws):
            at = s * ws + w
            eout[c * subs + s, w] = (far_slot[at] + dot_nn(oh_slot_bucket, shift[at])).astype(BF)

        @pl.when(level < last)
        def _():
            downward(c * subs + s).start()

    def deliver(c):
        @functools.partial(repeat, wc, unroll=8)
        def _(w):
            e_w = far[w] + dot_nn(oh_bucket_t, shift[w])
            ost[pl.ds(w, q, stride=wc), :] = e_w.T[0:q, :]

        out_v[c] = ost[...].reshape(q, wc, boxes).astype(BF)
        out_copy(c).start()

    @functools.partial(repeat, chunks)
    def _(c):
        near_field(c)

        @pl.when(carries[0] & (c == 0))
        def _():
            forward(0)
            for one in range(1, chunks):
                forward(one)
                send_direct(one)

        @functools.partial(repeat, nbox - 1)
        def _(j):
            from_peer(c, j + 1).wait_recv()

        own_copy(c).wait()
        far_field(c)

        for s in range(subs):
            descend(c, s)
        deliver(c)

    @functools.partial(repeat, chunks)
    def _(c):
        @functools.partial(repeat, nbox - 1)
        def _(j):
            exchange(c, j + 1).wait_send()

        for s in range(subs):
            @pl.when(level > 0)
            def _():
                upward(c * subs + s).wait_send()

            @pl.when(level < last)
            def _():
                downward(c * subs + s).wait_send()

        for r in range(len(relayed)):
            @pl.when(carries[r])
            def _():
                carry_on(c, r).wait_send()

        out_copy(c).wait()


def copy_kernel(parts, a_ref, b_ref, held, sems):
    size = a_ref.shape[0] // parts
    at = [pl.ds(i * size, size) for i in range(parts)]
    inward = [pltpu.make_async_copy(a_ref.at[at[i]], held.at[at[i]], sems.at[0, i]) for i in range(parts)]
    outward = [pltpu.make_async_copy(held.at[at[i]], b_ref.at[at[i]], sems.at[1, i]) for i in range(parts)]
    for one in inward:
        one.start()
    for i in range(parts):
        inward[i].wait()
        outward[i].start()
    for one in outward:
        one.wait()


def per_device(
    sources, upward_maps, downward_maps, cross_maps, child_octant, child_parent, parent_box,
    send_index, near_source, near_target, far_source, far_target,
):
    nbox, nleaf = lax.axis_size("box"), lax.axis_size("leaf")
    _, q, w_all, boxes = sources.shape
    par = parent_box.shape[1]
    rows_k = near_source.shape[2]
    pairs = near_source.shape[1] * rows_k
    wc, ws = 16, 4
    chunks, n_sub = w_all // wc, w_all // ws
    dims = (nbox, nleaf, q, w_all, boxes, par, wc, ws, rows_k)
    integers = (
        child_octant, child_parent, parent_box, send_index[0, 0].T,
        near_source[0], near_target[0], far_source[0], far_target[0],
    )
    dma = pltpu.SemaphoreType.DMA
    any_spec = pl.BlockSpec(memory_space=pl.ANY)
    n_cross = cross_maps.shape[0]
    out = pl.pallas_call(
        functools.partial(kernel, dims),
        out_shape=jax.ShapeDtypeStruct((q, w_all, boxes), BF),
        in_specs=[any_spec] * 12,
        out_specs=any_spec,
        scratch_shapes=[pltpu.VMEM(one.shape, jnp.int32) for one in integers]
        + [
            pltpu.VMEM((chunks, q, wc, boxes), BF),
            pltpu.VMEM(upward_maps.shape, BF),
            pltpu.VMEM(downward_maps.shape, BF),
            pltpu.VMEM(cross_maps.shape, BF),
            pltpu.VMEM((8, QP, QP), BF),
            pltpu.VMEM((8, QP, QP), BF),
            pltpu.VMEM((n_cross, QP, QP), BF),
            pltpu.VMEM((QP * wc, boxes), F32),
            pltpu.VMEM((w_all, boxes, QP), BF),
            pltpu.VMEM((wc, par, QP), F32),
            pltpu.VMEM((wc, 8 * par, QP), F32),
            pltpu.VMEM((ws, 8 * par, QP), BF),
            pltpu.VMEM((n_sub, ws, par, QP), BF),
            pltpu.VMEM((n_sub, ws, par, QP), BF),
            pltpu.VMEM((2 * CAP - 1, nbox * wc, 128), F32),
            pltpu.VMEM((chunks, nbox, (2 * CAP - 1) * wc, 128), BF),
            pltpu.VMEM((chunks, nbox, (2 * CAP - 1) * wc, 128), BF),
            pltpu.VMEM((wc, pairs, QP), BF),
            pltpu.VMEM((wc, pairs, QP), BF),
            pltpu.VMEM((wc, boxes, QP), F32),
            pltpu.VMEM((wc, par, QP), F32),
            pltpu.VMEM((n_sub, ws, par, QP), BF),
            pltpu.VMEM((n_sub, ws, par, QP), BF),
            pltpu.VMEM((wc, 8 * par, QP), BF),
            pltpu.VMEM((q * wc, boxes), F32),
            pltpu.VMEM((chunks, q, wc, boxes), BF),
            pltpu.VMEM((chunks, RELAYS[0], (2 * CAP - 1) * wc, 128), BF),
            dma((len(integers),)), dma((chunks + 3,)),
            dma((n_sub,)), dma((n_sub,)), dma((n_sub,)), dma((n_sub,)),
            dma((chunks, nbox)), dma((chunks, nbox)), dma((chunks,)), dma((chunks,)),
            dma((chunks, RELAYS[0])), dma((chunks, RELAYS[0])),
        ],
        compiler_params=pltpu.CompilerParams(
            collective_id=0, has_side_effects=True, vmem_limit_bytes=60 * 1024 * 1024
        ),
    )(
        sources[0], upward_maps, downward_maps, cross_maps, *integers
    )
    parts = 8
    out = pl.pallas_call(
        functools.partial(copy_kernel, parts),
        out_shape=jax.ShapeDtypeStruct((q, w_all, boxes), BF),
        in_specs=[any_spec],
        out_specs=any_spec,
        scratch_shapes=[pltpu.VMEM((q, w_all, boxes), BF), dma((2, parts))],
        compiler_params=pltpu.CompilerParams(vmem_limit_bytes=60 * 1024 * 1024),
    )(out)
    return out[None]


def solution(mesh):
    placed = (
        P("leaf", None, None, "box"),
        P(),
        P(),
        P(),
        P("leaf", "box"),
        P("leaf", "box"),
        P("leaf", "box"),
        P("leaf", "box", None, None),
        P("leaf", None, "box"),
        P("leaf", None, "box"),
        P("leaf", None, "box"),
        P("leaf", None, "box"),
    )
    return jax.shard_map(
        per_device,
        mesh=mesh,
        in_specs=placed,
        out_specs=P("leaf", None, None, "box"),
        check_vma=False,
    )
```

```python
import functools

import jax
import jax.numpy as jnp
from jax import lax
from jax.experimental import pallas as pl
from jax.experimental.pallas import tpu as pltpu
from jax.sharding import PartitionSpec as P

BF = jnp.bfloat16
F32 = jnp.float32
MESH = pl.DeviceIdType.MESH
QP = 256
CAP = 4
RELAYS = (3, 1)


def dot_nn(a, b):
    return lax.dot_general(a, b, (((1,), (0,)), ((), ())), preferred_element_type=F32)


def dot_nt(a, b):
    return lax.dot_general(a, b, (((1,), (1,)), ((), ())), preferred_element_type=F32)


def iota(shape, dim):
    return lax.broadcasted_iota(jnp.int32, shape, dim)


def onehot(mask):
    return mask.astype(F32).astype(BF)


def column_of(table, by_column):
    a, b = table.shape
    n = a * b
    row = iota((n, 1), 0)
    of_a, of_b = (row % a, row // a) if by_column else (row // b, row % b)
    picked = dot_nn(onehot(of_a == iota((n, a), 1)), table.astype(F32).astype(BF))
    return jnp.sum(jnp.where(of_b == iota((n, b), 1), picked, 0.0), axis=1, keepdims=True)


def is_at(column, width):
    return onehot(column == iota((column.shape[0], width), 1).astype(F32))


def repeat(count, body, unroll=1):
    def step(index, carry):
        body(index)
        return carry

    lax.fori_loop(0, count, step, 0, unroll=unroll)


def kernel(
    dims,
    x_hbm, up_hbm, down_hbm, cross_hbm, octant_hbm, parent_hbm, slots_hbm,
    send_index_hbm, near_src_hbm, near_dst_hbm, far_src_hbm, far_dst_hbm,
    out_hbm,
    octant_ref, parent_ref, slots_ref,
    send_index_ref, near_src_ref, near_dst_ref, far_src_ref, far_dst_ref,
    x_in, up_in, down_in, cross_in, up_maps, down_maps, cross_maps,
    x32, m_buf, x_slot, base, bucket, cin, cout, st, send, recv, gath, moved, far, far_slot,
    ein, eout, shift, ost, out_v, relay,
    sem_int, sem_in, sem_cs, sem_cr, sem_es, sem_er, sem_as, sem_ar, sem_own, sem_out, sem_rs, sem_rr,
):
    nbox, nleaf, q, w_all, boxes, par, wc, ws, rows_k = dims
    chunks, subs = w_all // wc, wc // ws
    rest = q - 128
    me = lax.axis_index("box")
    level = lax.axis_index("leaf")
    last = nleaf - 1
    mirror = nleaf - 2 - level // 2 * 2 + level % 2
    relayed = [nbox // 2, nbox // 2 + 1, nbox // 2 - 1][: RELAYS[0]]
    hands_over = [level < 2 * sum(n > r for n in RELAYS) for r in range(len(relayed))]
    carries = [level >= nleaf - 2 * sum(n > r for n in RELAYS) for r in range(len(relayed))]

    barrier = pltpu.get_barrier_semaphore()

    def greet_mirror(offset):
        pl.semaphore_signal(
            barrier, inc=1, device_id={"box": lax.rem(me + nbox + offset, nbox), "leaf": mirror},
            device_id_type=MESH,
        )

    def x_copy(c):
        return pltpu.make_async_copy(
            x_hbm.at[:, pl.ds(pl.multiple_of(c * wc, 16), wc), :], x_in.at[c], sem_in.at[c]
        )

    def out_copy(c):
        return pltpu.make_async_copy(
            out_v.at[c], out_hbm.at[:, pl.ds(pl.multiple_of(c * wc, 16), wc), :], sem_out.at[c]
        )

    copy_up = pltpu.make_async_copy(up_hbm, up_in, sem_in.at[chunks])
    copy_down = pltpu.make_async_copy(down_hbm, down_in, sem_in.at[chunks + 1])
    copy_cross = pltpu.make_async_copy(cross_hbm, cross_in, sem_in.at[chunks + 2])
    int_copies = [
        pltpu.make_async_copy(source, target, sem_int.at[i])
        for i, (source, target) in enumerate(
            (
                (octant_hbm, octant_ref), (parent_hbm, parent_ref), (slots_hbm, slots_ref),
                (send_index_hbm, send_index_ref), (near_src_hbm, near_src_ref),
                (near_dst_hbm, near_dst_ref), (far_src_hbm, far_src_ref), (far_dst_hbm, far_dst_ref),
            )
        )
    ]
    for one in int_copies:
        one.start()
    x_copy(0).start()
    copy_up.start()

    @pl.when(level > 0)
    def _():
        pl.semaphore_signal(barrier, inc=1, device_id={"leaf": level - 1}, device_id_type=MESH)

    @pl.when(level < last)
    def _():
        pl.semaphore_signal(barrier, inc=1, device_id={"leaf": level + 1}, device_id_type=MESH)

    @functools.partial(repeat, nbox - 1)
    def _(j):
        pl.semaphore_signal(
            barrier, inc=1, device_id={"box": lax.rem(me + j + 1, nbox)}, device_id_type=MESH
        )

    expected = nbox + 1 - (level == 0).astype(jnp.int32) - (level == last).astype(jnp.int32)
    for r, offset in enumerate(relayed):
        expected += (hands_over[r] | carries[r]).astype(jnp.int32) * (2 if r == 0 else 1)

        @pl.when(hands_over[r])
        def _():
            greet_mirror(-offset)
            if r == 0:
                greet_mirror(0)

        @pl.when(carries[r])
        def _():
            greet_mirror(offset)
            if r == 0:
                greet_mirror(0)

    for c in range(1, chunks):
        x_copy(c).start()
    copy_down.start()
    copy_cross.start()
    for one in int_copies:
        one.wait()

    bucket_row = octant_ref[...] * par + parent_ref[...]
    oh_bucket = onehot(bucket_row == iota((8 * par, boxes), 0))
    oh_slot = is_at(column_of(slots_ref[...], False), boxes)
    oh_slot_t = onehot(slots_ref[...] == iota((boxes, par), 0))
    in_slots = jnp.max(oh_slot.astype(F32), axis=0, keepdims=True)
    oh_bucket_base = (oh_bucket.astype(F32) * (1.0 - in_slots)).astype(BF)
    oh_bucket_slot = dot_nn(oh_bucket, oh_slot_t).astype(BF)
    oh_send = is_at(column_of(send_index_ref[...], False), boxes)

    def turn_maps(source, target, count):
        @functools.partial(repeat, count, unroll=2)
        def _(k):
            target[k] = jnp.zeros((QP, QP), BF)
            target[k, 0:q, 0:q] = source[k].astype(F32).T.astype(BF)

    @pl.when(level == last)
    def _():
        cin[...] = jnp.zeros_like(cin)

    @pl.when(level == 0)
    def _():
        ein[...] = jnp.zeros_like(ein)

    def chain(buf_from, buf_to, c, s_sem, r_sem, target):
        return pltpu.make_async_remote_copy(
            src_ref=buf_from.at[c], dst_ref=buf_to.at[c], send_sem=s_sem.at[c], recv_sem=r_sem.at[c],
            device_id={"leaf": target}, device_id_type=MESH,
        )

    def upward(c):
        return chain(cout, cin, c, sem_cs, sem_cr, jnp.maximum(level - 1, 0))

    def downward(c):
        return chain(eout, ein, c, sem_es, sem_er, jnp.minimum(level + 1, last))

    def exchange(c, j):
        to = lax.rem(me + j, nbox)
        return pltpu.make_async_remote_copy(
            src_ref=send.at[c, to], dst_ref=recv.at[c, me], send_sem=sem_as.at[c, j],
            recv_sem=sem_ar.at[c, j], device_id={"box": to}, device_id_type=MESH,
        )

    def from_peer(c, j):
        peer = lax.rem(me + nbox - j, nbox)
        return pltpu.make_async_remote_copy(
            src_ref=send.at[c, peer], dst_ref=recv.at[c, peer], send_sem=sem_as.at[c, j],
            recv_sem=sem_ar.at[c, j], device_id={"box": peer}, device_id_type=MESH,
        )

    def hand_over(c, r):
        to = lax.rem(me + relayed[r], nbox)
        return pltpu.make_async_remote_copy(
            src_ref=send.at[c, to], dst_ref=relay.at[c, r], send_sem=sem_as.at[c, relayed[r]],
            recv_sem=sem_rr.at[c, r], device_id={"leaf": mirror}, device_id_type=MESH,
        )

    def carry_on(c, r):
        to = lax.rem(me + relayed[r], nbox)
        return pltpu.make_async_remote_copy(
            src_ref=relay.at[c, r], dst_ref=recv.at[c, me], send_sem=sem_rs.at[c, r],
            recv_sem=sem_ar.at[c, relayed[r]], device_id={"box": to, "leaf": mirror}, device_id_type=MESH,
        )

    def forward(c):
        for r in range(len(relayed)):
            @pl.when(carries[r])
            def _():
                hand_over(c, r).wait_recv()
                carry_on(c, r).start()

    def own_copy(c):
        return pltpu.make_async_copy(send.at[c, me], recv.at[c, me], sem_own.at[c])

    x32[q * wc :, :] = jnp.zeros(((QP - q) * wc, boxes), F32)

    def prepare(c):
        x_copy(c).wait()
        x32[0 : q * wc, :] = x_in[c].astype(F32).reshape(q * wc, boxes)

        @functools.partial(repeat, wc, unroll=8)
        def _(w):
            x_w = x32[pl.ds(w, QP, stride=wc), :].T.astype(BF)
            m_buf[c * wc + w] = x_w
            x_slot[w] = dot_nn(oh_slot, x_w)
            base[w] = dot_nn(oh_bucket_base, x_w)

    def climb(c, s):
        @pl.when(level < last)
        def _():
            upward(c * subs + s).wait_recv()

        for w in range(ws):
            at = s * ws + w
            slot_w = (x_slot[at] + cin[c * subs + s, w].astype(F32)).astype(BF)
            bucket[w] = (base[at] + dot_nn(oh_bucket_slot, slot_w)).astype(BF)
        rows = jnp.concatenate(
            [bucket[:, o * par : (o + 1) * par, :].reshape(ws * par, QP) for o in range(8)], axis=1
        )
        total = dot_nn(rows, up_maps[...].reshape(8 * QP, QP))
        cout[c * subs + s] = total.astype(BF).reshape(ws, par, QP)

        @pl.when(level > 0)
        def _():
            upward(c * subs + s).start()

    lane = iota((nbox, 128), 1)

    def send_direct(c):
        @functools.partial(repeat, nbox - 1)
        def _(j):
            direct = j >= 0
            for r, offset in enumerate(relayed):
                direct &= jnp.logical_not(hands_over[r] & (j + 1 == offset))

            @pl.when(direct)
            def _():
                exchange(c, j + 1).start()

    def hand_out(c):
        @functools.partial(repeat, wc, unroll=8)
        def _(w):
            at = c * wc + w
            c_w = cin[c * subs + w // ws, w % ws]
            m_w = (m_buf[at].astype(F32) + dot_nn(oh_slot_t, c_w)).astype(BF)
            m_buf[at] = m_w
            o_w = dot_nn(oh_send, m_w)
            tails = []
            for i in range(CAP):
                part = o_w[i * nbox : (i + 1) * nbox]
                st[i, pl.ds(w, nbox, stride=wc), :] = part[:, 0:128]
                tail = part[:, 128:QP]
                tails.append(pltpu.roll(tail, (i * rest) % 128, 1) if i else tail)
            for t in range(CAP - 1):
                packed = jnp.where(lane < (t + 1) * rest - t * 128, tails[t], tails[t + 1])
                st[CAP + t, pl.ds(w, nbox, stride=wc), :] = packed

        for t in range(2 * CAP - 1):
            send[c, :, t * wc : (t + 1) * wc, :] = st[t].astype(BF).reshape(nbox, wc, 128)

        for r in range(len(relayed)):
            @pl.when(hands_over[r])
            def _():
                hand_over(c, r).start()

        @pl.when(jnp.logical_not(carries[0]) | (c == 0))
        def _():
            send_direct(c)

        own_copy(c).start()

    prepare(0)
    copy_up.wait()
    turn_maps(up_in, up_maps, 8)
    pl.semaphore_wait(barrier, expected)

    @functools.partial(repeat, chunks)
    def _(c):
        @pl.when(c > 0)
        def _():
            prepare(c)

        for s in range(subs):
            climb(c, s)
        hand_out(c)

    oh_near_src = is_at(column_of(near_src_ref[...], False), boxes)
    far_src = far_src_ref[...]
    oh_far_src = is_at(column_of((far_src % CAP) * nbox + far_src // CAP, False), CAP * nbox)
    near_dst = is_at(column_of(near_dst_ref[...], False), boxes).astype(F32)
    far_dst = is_at(column_of(far_dst_ref[...], False), boxes).astype(F32)
    oh_near_dst = near_dst.T.astype(BF)
    oh_far_dst = far_dst.T.astype(BF)
    oh_near_slot = dot_nn(oh_slot, oh_near_dst).astype(BF)
    oh_far_slot = dot_nn(oh_slot, oh_far_dst).astype(BF)
    oh_bucket_t = oh_bucket.astype(F32).T.astype(BF)
    oh_slot_bucket = dot_nn(oh_slot, oh_bucket_t).astype(BF)
    copy_down.wait()
    turn_maps(down_in, down_maps, 8)
    copy_cross.wait()
    turn_maps(cross_in, cross_maps, cross_in.shape[0])

    def apply_cross():
        @functools.partial(repeat, cross_in.shape[0], unroll=4)
        def _(k):
            at = pl.ds(pl.multiple_of(k * rows_k, 16), rows_k)
            moved[:, at, :] = (
                dot_nn(gath[:, at, :].reshape(wc * rows_k, QP), cross_maps[k])
                .astype(BF)
                .reshape(wc, rows_k, QP)
            )

    def near_field(c):
        @functools.partial(repeat, wc, unroll=8)
        def _(w):
            gath[w] = dot_nn(oh_near_src, m_buf[c * wc + w]).astype(BF)

        apply_cross()

        @functools.partial(repeat, wc, unroll=8)
        def _(w):
            far[w] = dot_nn(oh_near_dst, moved[w])
            far_slot[w] = dot_nn(oh_near_slot, moved[w])

    def far_field(c):
        for t in range(2 * CAP - 1):
            st[t] = recv[c, :, t * wc : (t + 1) * wc, :].astype(F32).reshape(nbox * wc, 128)

        @functools.partial(repeat, wc, unroll=8)
        def _(w):
            tiles = [st[t, pl.ds(w, nbox, stride=wc), :] for t in range(2 * CAP - 1)]
            parts = []
            for i in range(CAP):
                if i == 0:
                    tail = tiles[CAP]
                else:
                    tail = tiles[CAP + i - 1]
                    if i < CAP - 1:
                        tail = jnp.where(lane >= i * rest - (i - 1) * 128, tail, tiles[CAP + i])
                    tail = pltpu.roll(tail, (-i * rest) % 128, 1)
                tail = jnp.where(lane < rest, tail, 0.0)
                parts.append(jnp.concatenate([tiles[i], tail], axis=1))
            gath[w] = dot_nn(oh_far_src, jnp.concatenate(parts, axis=0).astype(BF)).astype(BF)

        apply_cross()

        @functools.partial(repeat, wc, unroll=8)
        def _(w):
            far[w] += dot_nn(oh_far_dst, moved[w])
            far_slot[w] += dot_nn(oh_far_slot, moved[w])

    def descend(c, s):
        @pl.when(level > 0)
        def _():
            downward(c * subs + s).wait_recv()

        rows = ein[c * subs + s].reshape(ws * par, QP)
        for o in range(8):
            shift[s * ws : (s + 1) * ws, o * par : (o + 1) * par, :] = (
                dot_nn(rows, down_maps[o]).astype(BF).reshape(ws, par, QP)
            )
        for w in range(ws):
            at = s * ws + w
            eout[c * subs + s, w] = (far_slot[at] + dot_nn(oh_slot_bucket, shift[at])).astype(BF)

        @pl.when(level < last)
        def _():
            downward(c * subs + s).start()

    def deliver(c):
        @functools.partial(repeat, wc, unroll=8)
        def _(w):
            e_w = far[w] + dot_nn(oh_bucket_t, shift[w])
            ost[pl.ds(w, q, stride=wc), :] = e_w.T[0:q, :]

        out_v[c] = ost[...].reshape(q, wc, boxes).astype(BF)
        out_copy(c).start()

    def settle(c):
        @functools.partial(repeat, nbox - 1)
        def _(j):
            exchange(c, j + 1).wait_send()

        for s in range(subs):
            @pl.when(level > 0)
            def _():
                upward(c * subs + s).wait_send()

        for r in range(len(relayed)):
            @pl.when(carries[r])
            def _():
                carry_on(c, r).wait_send()

    @functools.partial(repeat, chunks)
    def _(c):
        near_field(c)

        @pl.when(carries[0] & (c == 0))
        def _():
            forward(0)
            for one in range(1, chunks):
                forward(one)
                send_direct(one)

        @functools.partial(repeat, nbox - 1)
        def _(j):
            from_peer(c, j + 1).wait_recv()

        own_copy(c).wait()
        far_field(c)

        @pl.when(level >= nleaf // 2)
        def _():
            settle(c)

        for s in range(subs):
            descend(c, s)
        deliver(c)

        @pl.when(level < nleaf // 2)
        def _():
            settle(c)

    @functools.partial(repeat, chunks)
    def _(c):
        for s in range(subs):
            @pl.when(level < last)
            def _():
                downward(c * subs + s).wait_send()

        out_copy(c).wait()


def copy_kernel(parts, a_ref, b_ref, held, sems):
    size = a_ref.shape[0] // parts
    at = [pl.ds(i * size, size) for i in range(parts)]
    inward = [pltpu.make_async_copy(a_ref.at[at[i]], held.at[at[i]], sems.at[0, i]) for i in range(parts)]
    outward = [pltpu.make_async_copy(held.at[at[i]], b_ref.at[at[i]], sems.at[1, i]) for i in range(parts)]
    for one in inward:
        one.start()
    for i in range(parts):
        inward[i].wait()
        outward[i].start()
    for one in outward:
        one.wait()


def per_device(
    sources, upward_maps, downward_maps, cross_maps, child_octant, child_parent, parent_box,
    send_index, near_source, near_target, far_source, far_target,
):
    nbox, nleaf = lax.axis_size("box"), lax.axis_size("leaf")
    _, q, w_all, boxes = sources.shape
    par = parent_box.shape[1]
    rows_k = near_source.shape[2]
    pairs = near_source.shape[1] * rows_k
    wc, ws = 16, 4
    chunks, n_sub = w_all // wc, w_all // ws
    dims = (nbox, nleaf, q, w_all, boxes, par, wc, ws, rows_k)
    integers = (
        child_octant, child_parent, parent_box, send_index[0, 0].T,
        near_source[0], near_target[0], far_source[0], far_target[0],
    )
    dma = pltpu.SemaphoreType.DMA
    any_spec = pl.BlockSpec(memory_space=pl.ANY)
    n_cross = cross_maps.shape[0]
    out = pl.pallas_call(
        functools.partial(kernel, dims),
        out_shape=jax.ShapeDtypeStruct((q, w_all, boxes), BF),
        in_specs=[any_spec] * 12,
        out_specs=any_spec,
        scratch_shapes=[pltpu.VMEM(one.shape, jnp.int32) for one in integers]
        + [
            pltpu.VMEM((chunks, q, wc, boxes), BF),
            pltpu.VMEM(upward_maps.shape, BF),
            pltpu.VMEM(downward_maps.shape, BF),
            pltpu.VMEM(cross_maps.shape, BF),
            pltpu.VMEM((8, QP, QP), BF),
            pltpu.VMEM((8, QP, QP), BF),
            pltpu.VMEM((n_cross, QP, QP), BF),
            pltpu.VMEM((QP * wc, boxes), F32),
            pltpu.VMEM((w_all, boxes, QP), BF),
            pltpu.VMEM((wc, par, QP), F32),
            pltpu.VMEM((wc, 8 * par, QP), F32),
            pltpu.VMEM((ws, 8 * par, QP), BF),
            pltpu.VMEM((n_sub, ws, par, QP), BF),
            pltpu.VMEM((n_sub, ws, par, QP), BF),
            pltpu.VMEM((2 * CAP - 1, nbox * wc, 128), F32),
            pltpu.VMEM((chunks, nbox, (2 * CAP - 1) * wc, 128), BF),
            pltpu.VMEM((chunks, nbox, (2 * CAP - 1) * wc, 128), BF),
            pltpu.VMEM((wc, pairs, QP), BF),
            pltpu.VMEM((wc, pairs, QP), BF),
            pltpu.VMEM((wc, boxes, QP), F32),
            pltpu.VMEM((wc, par, QP), F32),
            pltpu.VMEM((n_sub, ws, par, QP), BF),
            pltpu.VMEM((n_sub, ws, par, QP), BF),
            pltpu.VMEM((wc, 8 * par, QP), BF),
            pltpu.VMEM((q * wc, boxes), F32),
            pltpu.VMEM((chunks, q, wc, boxes), BF),
            pltpu.VMEM((chunks, RELAYS[0], (2 * CAP - 1) * wc, 128), BF),
            dma((len(integers),)), dma((chunks + 3,)),
            dma((n_sub,)), dma((n_sub,)), dma((n_sub,)), dma((n_sub,)),
            dma((chunks, nbox)), dma((chunks, nbox)), dma((chunks,)), dma((chunks,)),
            dma((chunks, RELAYS[0])), dma((chunks, RELAYS[0])),
        ],
        compiler_params=pltpu.CompilerParams(
            collective_id=0, has_side_effects=True, vmem_limit_bytes=60 * 1024 * 1024
        ),
    )(
        sources[0], upward_maps, downward_maps, cross_maps, *integers
    )
    parts = 8
    out = pl.pallas_call(
        functools.partial(copy_kernel, parts),
        out_shape=jax.ShapeDtypeStruct((q, w_all, boxes), BF),
        in_specs=[any_spec],
        out_specs=any_spec,
        scratch_shapes=[pltpu.VMEM((q, w_all, boxes), BF), dma((2, parts))],
        compiler_params=pltpu.CompilerParams(vmem_limit_bytes=60 * 1024 * 1024),
    )(out)
    return out[None]


def solution(mesh):
    placed = (
        P("leaf", None, None, "box"),
        P(),
        P(),
        P(),
        P("leaf", "box"),
        P("leaf", "box"),
        P("leaf", "box"),
        P("leaf", "box", None, None),
        P("leaf", None, "box"),
        P("leaf", None, "box"),
        P("leaf", None, "box"),
        P("leaf", None, "box"),
    )
    return jax.shard_map(
        per_device,
        mesh=mesh,
        in_specs=placed,
        out_specs=P("leaf", None, None, "box"),
        check_vma=False,
    )
```

```python
import functools

import jax
import jax.numpy as jnp
from jax import lax
from jax.experimental import pallas as pl
from jax.experimental.pallas import tpu as pltpu
from jax.sharding import PartitionSpec as P

BF = jnp.bfloat16
F32 = jnp.float32
MESH = pl.DeviceIdType.MESH
QP = 256
CAP = 4
RELAYS = (3, 1)


def dot_nn(a, b):
    return lax.dot_general(a, b, (((1,), (0,)), ((), ())), preferred_element_type=F32)


def dot_nt(a, b):
    return lax.dot_general(a, b, (((1,), (1,)), ((), ())), preferred_element_type=F32)


def iota(shape, dim):
    return lax.broadcasted_iota(jnp.int32, shape, dim)


def onehot(mask):
    return mask.astype(F32).astype(BF)


def column_of(table, by_column):
    a, b = table.shape
    n = a * b
    row = iota((n, 1), 0)
    of_a, of_b = (row % a, row // a) if by_column else (row // b, row % b)
    picked = dot_nn(onehot(of_a == iota((n, a), 1)), table.astype(F32).astype(BF))
    return jnp.sum(jnp.where(of_b == iota((n, b), 1), picked, 0.0), axis=1, keepdims=True)


def is_at(column, width):
    return onehot(column == iota((column.shape[0], width), 1).astype(F32))


def repeat(count, body, unroll=1):
    def step(index, carry):
        body(index)
        return carry

    lax.fori_loop(0, count, step, 0, unroll=unroll)


def kernel(
    dims,
    x_hbm, up_hbm, down_hbm, cross_hbm, octant_hbm, parent_hbm, slots_hbm,
    send_index_hbm, near_src_hbm, near_dst_hbm, far_src_hbm, far_dst_hbm,
    out_hbm,
    octant_ref, parent_ref, slots_ref,
    send_index_ref, near_src_ref, near_dst_ref, far_src_ref, far_dst_ref,
    x_in, up_in, down_in, cross_in, up_maps, down_maps, cross_maps,
    x32, m_buf, x_slot, base, bucket, cin, cout, st, send, recv, gath, moved, far, far_slot,
    ein, eout, shift, ost, out_v, relay,
    sem_int, sem_in, sem_cs, sem_cr, sem_es, sem_er, sem_as, sem_ar, sem_own, sem_out, sem_rs, sem_rr,
):
    nbox, nleaf, q, w_all, boxes, par, wc, ws, rows_k = dims
    chunks, subs = w_all // wc, wc // ws
    rest = q - 128
    me = lax.axis_index("box")
    level = lax.axis_index("leaf")
    last = nleaf - 1
    mirror = nleaf - 2 - level // 2 * 2 + level % 2
    relayed = [nbox // 2, nbox // 2 + 1, nbox // 2 - 1][: RELAYS[0]]
    hands_over = [level < 2 * sum(n > r for n in RELAYS) for r in range(len(relayed))]
    carries = [level >= nleaf - 2 * sum(n > r for n in RELAYS) for r in range(len(relayed))]

    barrier = pltpu.get_barrier_semaphore()

    def greet_mirror(offset):
        pl.semaphore_signal(
            barrier, inc=1, device_id={"box": lax.rem(me + nbox + offset, nbox), "leaf": mirror},
            device_id_type=MESH,
        )

    def x_copy(c):
        return pltpu.make_async_copy(
            x_hbm.at[:, pl.ds(pl.multiple_of(c * wc, 16), wc), :], x_in.at[c], sem_in.at[c]
        )

    def out_copy(c):
        return pltpu.make_async_copy(
            out_v.at[c], out_hbm.at[:, pl.ds(pl.multiple_of(c * wc, 16), wc), :], sem_out.at[c]
        )

    copy_up = pltpu.make_async_copy(up_hbm, up_in, sem_in.at[chunks])
    copy_down = pltpu.make_async_copy(down_hbm, down_in, sem_in.at[chunks + 1])
    copy_cross = pltpu.make_async_copy(cross_hbm, cross_in, sem_in.at[chunks + 2])
    int_copies = [
        pltpu.make_async_copy(source, target, sem_int.at[i])
        for i, (source, target) in enumerate(
            (
                (octant_hbm, octant_ref), (parent_hbm, parent_ref), (slots_hbm, slots_ref),
                (send_index_hbm, send_index_ref), (near_src_hbm, near_src_ref),
                (near_dst_hbm, near_dst_ref), (far_src_hbm, far_src_ref), (far_dst_hbm, far_dst_ref),
            )
        )
    ]
    for one in int_copies:
        one.start()
    x_copy(0).start()
    copy_up.start()

    @pl.when(level > 0)
    def _():
        pl.semaphore_signal(barrier, inc=1, device_id={"leaf": level - 1}, device_id_type=MESH)

    @pl.when(level < last)
    def _():
        pl.semaphore_signal(barrier, inc=1, device_id={"leaf": level + 1}, device_id_type=MESH)

    @functools.partial(repeat, nbox - 1)
    def _(j):
        pl.semaphore_signal(
            barrier, inc=1, device_id={"box": lax.rem(me + j + 1, nbox)}, device_id_type=MESH
        )

    expected = nbox + 1 - (level == 0).astype(jnp.int32) - (level == last).astype(jnp.int32)
    for r, offset in enumerate(relayed):
        expected += (hands_over[r] | carries[r]).astype(jnp.int32) * (2 if r == 0 else 1)

        @pl.when(hands_over[r])
        def _():
            greet_mirror(-offset)
            if r == 0:
                greet_mirror(0)

        @pl.when(carries[r])
        def _():
            greet_mirror(offset)
            if r == 0:
                greet_mirror(0)

    for c in range(1, chunks):
        x_copy(c).start()
    copy_down.start()
    copy_cross.start()
    for one in int_copies:
        one.wait()

    bucket_row = octant_ref[...] * par + parent_ref[...]
    oh_bucket = onehot(bucket_row == iota((8 * par, boxes), 0))
    oh_slot = is_at(column_of(slots_ref[...], False), boxes)
    oh_slot_t = onehot(slots_ref[...] == iota((boxes, par), 0))
    in_slots = jnp.max(oh_slot.astype(F32), axis=0, keepdims=True)
    oh_bucket_base = (oh_bucket.astype(F32) * (1.0 - in_slots)).astype(BF)
    oh_bucket_slot = dot_nn(oh_bucket, oh_slot_t).astype(BF)
    oh_send = is_at(column_of(send_index_ref[...], False), boxes)

    def turn_maps(source, target, count):
        @functools.partial(repeat, count, unroll=2)
        def _(k):
            target[k] = jnp.zeros((QP, QP), BF)
            target[k, 0:q, 0:q] = source[k].astype(F32).T.astype(BF)

    @pl.when(level == last)
    def _():
        cin[...] = jnp.zeros_like(cin)

    @pl.when(level == 0)
    def _():
        ein[...] = jnp.zeros_like(ein)

    def chain(buf_from, buf_to, c, s_sem, r_sem, target):
        return pltpu.make_async_remote_copy(
            src_ref=buf_from.at[c], dst_ref=buf_to.at[c], send_sem=s_sem.at[c], recv_sem=r_sem.at[c],
            device_id={"leaf": target}, device_id_type=MESH,
        )

    def upward(c):
        return chain(cout, cin, c, sem_cs, sem_cr, jnp.maximum(level - 1, 0))

    def downward(c):
        return chain(eout, ein, c, sem_es, sem_er, jnp.minimum(level + 1, last))

    def exchange(c, j):
        to = lax.rem(me + j, nbox)
        return pltpu.make_async_remote_copy(
            src_ref=send.at[c, to], dst_ref=recv.at[c, me], send_sem=sem_as.at[c, j],
            recv_sem=sem_ar.at[c, j], device_id={"box": to}, device_id_type=MESH,
        )

    def from_peer(c, j):
        peer = lax.rem(me + nbox - j, nbox)
        return pltpu.make_async_remote_copy(
            src_ref=send.at[c, peer], dst_ref=recv.at[c, peer], send_sem=sem_as.at[c, j],
            recv_sem=sem_ar.at[c, j], device_id={"box": peer}, device_id_type=MESH,
        )

    def in_chunk(c, r):
        return jnp.asarray(c < chunks - 1) | (r < 2)

    def hand_over(c, r):
        to = lax.rem(me + relayed[r], nbox)
        return pltpu.make_async_remote_copy(
            src_ref=send.at[c, to], dst_ref=relay.at[c, r], send_sem=sem_as.at[c, relayed[r]],
            recv_sem=sem_rr.at[c, r], device_id={"leaf": mirror}, device_id_type=MESH,
        )

    def carry_on(c, r):
        to = lax.rem(me + relayed[r], nbox)
        return pltpu.make_async_remote_copy(
            src_ref=relay.at[c, r], dst_ref=recv.at[c, me], send_sem=sem_rs.at[c, r],
            recv_sem=sem_ar.at[c, relayed[r]], device_id={"box": to, "leaf": mirror}, device_id_type=MESH,
        )

    def forward(c):
        for r in range(len(relayed)):
            @pl.when(carries[r] & in_chunk(c, r))
            def _():
                hand_over(c, r).wait_recv()
                carry_on(c, r).start()

    def own_copy(c):
        return pltpu.make_async_copy(send.at[c, me], recv.at[c, me], sem_own.at[c])

    x32[q * wc :, :] = jnp.zeros(((QP - q) * wc, boxes), F32)

    def prepare(c):
        x_copy(c).wait()
        x32[0 : q * wc, :] = x_in[c].astype(F32).reshape(q * wc, boxes)

        @functools.partial(repeat, wc, unroll=8)
        def _(w):
            x_w = x32[pl.ds(w, QP, stride=wc), :].T.astype(BF)
            m_buf[c * wc + w] = x_w
            x_slot[w] = dot_nn(oh_slot, x_w)
            base[w] = dot_nn(oh_bucket_base, x_w)

    def climb(c, s):
        @pl.when(level < last)
        def _():
            upward(c * subs + s).wait_recv()

        for w in range(ws):
            at = s * ws + w
            slot_w = (x_slot[at] + cin[c * subs + s, w].astype(F32)).astype(BF)
            bucket[w] = (base[at] + dot_nn(oh_bucket_slot, slot_w)).astype(BF)
        rows = jnp.concatenate(
            [bucket[:, o * par : (o + 1) * par, :].reshape(ws * par, QP) for o in range(8)], axis=1
        )
        total = dot_nn(rows, up_maps[...].reshape(8 * QP, QP))
        cout[c * subs + s] = total.astype(BF).reshape(ws, par, QP)

        @pl.when(level > 0)
        def _():
            upward(c * subs + s).start()

    lane = iota((nbox, 128), 1)

    def send_direct(c):
        @functools.partial(repeat, nbox - 1)
        def _(j):
            direct = j >= 0
            for r, offset in enumerate(relayed):
                direct &= jnp.logical_not(hands_over[r] & in_chunk(c, r) & (j + 1 == offset))

            @pl.when(direct)
            def _():
                exchange(c, j + 1).start()

    def hand_out(c):
        @functools.partial(repeat, wc, unroll=8)
        def _(w):
            at = c * wc + w
            c_w = cin[c * subs + w // ws, w % ws]
            m_w = (m_buf[at].astype(F32) + dot_nn(oh_slot_t, c_w)).astype(BF)
            m_buf[at] = m_w
            o_w = dot_nn(oh_send, m_w)
            tails = []
            for i in range(CAP):
                part = o_w[i * nbox : (i + 1) * nbox]
                st[i, pl.ds(w, nbox, stride=wc), :] = part[:, 0:128]
                tail = part[:, 128:QP]
                tails.append(pltpu.roll(tail, (i * rest) % 128, 1) if i else tail)
            for t in range(CAP - 1):
                packed = jnp.where(lane < (t + 1) * rest - t * 128, tails[t], tails[t + 1])
                st[CAP + t, pl.ds(w, nbox, stride=wc), :] = packed

        for t in range(2 * CAP - 1):
            send[c, :, t * wc : (t + 1) * wc, :] = st[t].astype(BF).reshape(nbox, wc, 128)

        for r in range(len(relayed)):
            @pl.when(hands_over[r] & in_chunk(c, r))
            def _():
                hand_over(c, r).start()

        @pl.when(jnp.logical_not(carries[0]) | (c == 0))
        def _():
            send_direct(c)

        own_copy(c).start()

    prepare(0)
    copy_up.wait()
    turn_maps(up_in, up_maps, 8)
    pl.semaphore_wait(barrier, expected)

    @functools.partial(repeat, chunks)
    def _(c):
        @pl.when(c > 0)
        def _():
            prepare(c)

        for s in range(subs):
            climb(c, s)
        hand_out(c)

    oh_near_src = is_at(column_of(near_src_ref[...], False), boxes)
    far_src = far_src_ref[...]
    oh_far_src = is_at(column_of((far_src % CAP) * nbox + far_src // CAP, False), CAP * nbox)
    near_dst = is_at(column_of(near_dst_ref[...], False), boxes).astype(F32)
    far_dst = is_at(column_of(far_dst_ref[...], False), boxes).astype(F32)
    oh_near_dst = near_dst.T.astype(BF)
    oh_far_dst = far_dst.T.astype(BF)
    oh_near_slot = dot_nn(oh_slot, oh_near_dst).astype(BF)
    oh_far_slot = dot_nn(oh_slot, oh_far_dst).astype(BF)
    oh_bucket_t = oh_bucket.astype(F32).T.astype(BF)
    slot_bucket = jnp.sum(oh_slot.astype(F32) * bucket_row.astype(F32), axis=1, keepdims=True)
    pick_at = (iota((8 * par, par), 0) // par * par + iota((8 * par, par), 1)).astype(F32)
    oh_pick = onehot(jnp.concatenate([slot_bucket] * 8, axis=0) == pick_at)
    copy_down.wait()
    turn_maps(down_in, down_maps, 8)
    copy_cross.wait()
    turn_maps(cross_in, cross_maps, cross_in.shape[0])

    def apply_cross():
        @functools.partial(repeat, cross_in.shape[0], unroll=4)
        def _(k):
            at = pl.ds(pl.multiple_of(k * rows_k, 16), rows_k)
            moved[:, at, :] = (
                dot_nn(gath[:, at, :].reshape(wc * rows_k, QP), cross_maps[k])
                .astype(BF)
                .reshape(wc, rows_k, QP)
            )

    def near_field(c):
        @functools.partial(repeat, wc, unroll=8)
        def _(w):
            gath[w] = dot_nn(oh_near_src, m_buf[c * wc + w]).astype(BF)

        apply_cross()

        @functools.partial(repeat, wc, unroll=8)
        def _(w):
            far[w] = dot_nn(oh_near_dst, moved[w])
            far_slot[w] = dot_nn(oh_near_slot, moved[w])

    def far_field(c):
        for t in range(2 * CAP - 1):
            st[t] = recv[c, :, t * wc : (t + 1) * wc, :].astype(F32).reshape(nbox * wc, 128)

        @functools.partial(repeat, wc, unroll=8)
        def _(w):
            tiles = [st[t, pl.ds(w, nbox, stride=wc), :] for t in range(2 * CAP - 1)]
            parts = []
            for i in range(CAP):
                if i == 0:
                    tail = tiles[CAP]
                else:
                    tail = tiles[CAP + i - 1]
                    if i < CAP - 1:
                        tail = jnp.where(lane >= i * rest - (i - 1) * 128, tail, tiles[CAP + i])
                    tail = pltpu.roll(tail, (-i * rest) % 128, 1)
                tail = jnp.where(lane < rest, tail, 0.0)
                parts.append(jnp.concatenate([tiles[i], tail], axis=1))
            gath[w] = dot_nn(oh_far_src, jnp.concatenate(parts, axis=0).astype(BF)).astype(BF)

        apply_cross()

        @functools.partial(repeat, wc, unroll=8)
        def _(w):
            far[w] += dot_nn(oh_far_dst, moved[w])
            far_slot[w] += dot_nn(oh_far_slot, moved[w])

    def descend(c, s):
        @pl.when(level > 0)
        def _():
            downward(c * subs + s).wait_recv()

        @pl.when(level < last)
        def _():
            for w in range(ws):
                bucket[w] = dot_nn(oh_pick, ein[c * subs + s, w]).astype(BF)
            rows = jnp.concatenate(
                [bucket[:, o * par : (o + 1) * par, :].reshape(ws * par, QP) for o in range(8)], axis=1
            )
            total = dot_nn(rows, down_maps[...].reshape(8 * QP, QP))
            held = far_slot[s * ws : (s + 1) * ws].reshape(ws * par, QP)
            eout[c * subs + s] = (held + total).astype(BF).reshape(ws, par, QP)
            downward(c * subs + s).start()

    def deliver(c):
        rows = ein[pl.ds(c * subs, subs)].reshape(wc * par, QP)
        for o in range(8):
            shift[:, o * par : (o + 1) * par, :] = (
                dot_nn(rows, down_maps[o]).astype(BF).reshape(wc, par, QP)
            )

        @functools.partial(repeat, wc, unroll=8)
        def _(w):
            e_w = far[w] + dot_nn(oh_bucket_t, shift[w])
            ost[pl.ds(w, q, stride=wc), :] = e_w.T[0:q, :]

        out_v[c] = ost[...].reshape(q, wc, boxes).astype(BF)
        out_copy(c).start()

    def settle(c):
        @functools.partial(repeat, nbox - 1)
        def _(j):
            exchange(c, j + 1).wait_send()

        for s in range(subs):
            @pl.when(level > 0)
            def _():
                upward(c * subs + s).wait_send()

        for r in range(len(relayed)):
            @pl.when(carries[r] & in_chunk(c, r))
            def _():
                carry_on(c, r).wait_send()

    @functools.partial(repeat, chunks)
    def _(c):
        near_field(c)

        @pl.when(carries[0] & (c == 0))
        def _():
            forward(0)
            for one in range(1, chunks):
                forward(one)
                send_direct(one)

        @functools.partial(repeat, nbox - 1)
        def _(j):
            from_peer(c, j + 1).wait_recv()

        own_copy(c).wait()
        far_field(c)

        @pl.when(level >= nleaf // 2)
        def _():
            settle(c)

        for s in range(subs):
            descend(c, s)
        deliver(c)

        @pl.when(level < nleaf // 2)
        def _():
            settle(c)

    @functools.partial(repeat, chunks)
    def _(c):
        for s in range(subs):
            @pl.when(level < last)
            def _():
                downward(c * subs + s).wait_send()

        out_copy(c).wait()


def copy_kernel(parts, a_ref, b_ref, held, sems):
    size = a_ref.shape[0] // parts
    at = [pl.ds(i * size, size) for i in range(parts)]
    inward = [pltpu.make_async_copy(a_ref.at[at[i]], held.at[at[i]], sems.at[0, i]) for i in range(parts)]
    outward = [pltpu.make_async_copy(held.at[at[i]], b_ref.at[at[i]], sems.at[1, i]) for i in range(parts)]
    for one in inward:
        one.start()
    for i in range(parts):
        inward[i].wait()
        outward[i].start()
    for one in outward:
        one.wait()


def per_device(
    sources, upward_maps, downward_maps, cross_maps, child_octant, child_parent, parent_box,
    send_index, near_source, near_target, far_source, far_target,
):
    nbox, nleaf = lax.axis_size("box"), lax.axis_size("leaf")
    _, q, w_all, boxes = sources.shape
    par = parent_box.shape[1]
    rows_k = near_source.shape[2]
    pairs = near_source.shape[1] * rows_k
    wc, ws = 16, 4
    chunks, n_sub = w_all // wc, w_all // ws
    dims = (nbox, nleaf, q, w_all, boxes, par, wc, ws, rows_k)
    integers = (
        child_octant, child_parent, parent_box, send_index[0, 0].T,
        near_source[0], near_target[0], far_source[0], far_target[0],
    )
    dma = pltpu.SemaphoreType.DMA
    any_spec = pl.BlockSpec(memory_space=pl.ANY)
    n_cross = cross_maps.shape[0]
    out = pl.pallas_call(
        functools.partial(kernel, dims),
        out_shape=jax.ShapeDtypeStruct((q, w_all, boxes), BF),
        in_specs=[any_spec] * 12,
        out_specs=any_spec,
        scratch_shapes=[pltpu.VMEM(one.shape, jnp.int32) for one in integers]
        + [
            pltpu.VMEM((chunks, q, wc, boxes), BF),
            pltpu.VMEM(upward_maps.shape, BF),
            pltpu.VMEM(downward_maps.shape, BF),
            pltpu.VMEM(cross_maps.shape, BF),
            pltpu.VMEM((8, QP, QP), BF),
            pltpu.VMEM((8, QP, QP), BF),
            pltpu.VMEM((n_cross, QP, QP), BF),
            pltpu.VMEM((QP * wc, boxes), F32),
            pltpu.VMEM((w_all, boxes, QP), BF),
            pltpu.VMEM((wc, par, QP), F32),
            pltpu.VMEM((wc, 8 * par, QP), F32),
            pltpu.VMEM((ws, 8 * par, QP), BF),
            pltpu.VMEM((n_sub, ws, par, QP), BF),
            pltpu.VMEM((n_sub, ws, par, QP), BF),
            pltpu.VMEM((2 * CAP - 1, nbox * wc, 128), F32),
            pltpu.VMEM((chunks, nbox, (2 * CAP - 1) * wc, 128), BF),
            pltpu.VMEM((chunks, nbox, (2 * CAP - 1) * wc, 128), BF),
            pltpu.VMEM((wc, pairs, QP), BF),
            pltpu.VMEM((wc, pairs, QP), BF),
            pltpu.VMEM((wc, boxes, QP), F32),
            pltpu.VMEM((wc, par, QP), F32),
            pltpu.VMEM((n_sub, ws, par, QP), BF),
            pltpu.VMEM((n_sub, ws, par, QP), BF),
            pltpu.VMEM((wc, 8 * par, QP), BF),
            pltpu.VMEM((q * wc, boxes), F32),
            pltpu.VMEM((chunks, q, wc, boxes), BF),
            pltpu.VMEM((chunks, RELAYS[0], (2 * CAP - 1) * wc, 128), BF),
            dma((len(integers),)), dma((chunks + 3,)),
            dma((n_sub,)), dma((n_sub,)), dma((n_sub,)), dma((n_sub,)),
            dma((chunks, nbox)), dma((chunks, nbox)), dma((chunks,)), dma((chunks,)),
            dma((chunks, RELAYS[0])), dma((chunks, RELAYS[0])),
        ],
        compiler_params=pltpu.CompilerParams(
            collective_id=0, has_side_effects=True, vmem_limit_bytes=60 * 1024 * 1024
        ),
    )(
        sources[0], upward_maps, downward_maps, cross_maps, *integers
    )
    parts = 8
    out = pl.pallas_call(
        functools.partial(copy_kernel, parts),
        out_shape=jax.ShapeDtypeStruct((q, w_all, boxes), BF),
        in_specs=[any_spec],
        out_specs=any_spec,
        scratch_shapes=[pltpu.VMEM((q, w_all, boxes), BF), dma((2, parts))],
        compiler_params=pltpu.CompilerParams(vmem_limit_bytes=60 * 1024 * 1024),
    )(out)
    return out[None]


def solution(mesh):
    placed = (
        P("leaf", None, None, "box"),
        P(),
        P(),
        P(),
        P("leaf", "box"),
        P("leaf", "box"),
        P("leaf", "box"),
        P("leaf", "box", None, None),
        P("leaf", None, "box"),
        P("leaf", None, "box"),
        P("leaf", None, "box"),
        P("leaf", None, "box"),
    )
    return jax.shard_map(
        per_device,
        mesh=mesh,
        in_specs=placed,
        out_specs=P("leaf", None, None, "box"),
        check_vma=False,
    )
```
